128 devices in a mesh: band: 2 (over x_lo), brick: 64 (over z, x_hi, y, core).
Axes of the slice: x: 4 (x_hi: 2, x_lo: 2; x = x_hi * 2 + x_lo), y: 4, z: 4, core: 2. Of those that a mesh axis runs over, the one named last changes fastest.
Arguments:
- stiffness: float32 [16, 2048, 128], P('band', 'brick'), may hold values from 0.5 to 8
- prescribed: float32 [3, 16, 2048, 128], P(None, 'band', 'brick'), may hold values from -6 to 6
- pinned: int32 [16, 2048, 128], P('band', 'brick'), may hold values 0 or 1
Outputs:
- displacement: float32 [3, 16, 2048, 128], P(None, 'band', 'brick')
The draws below stay inside these ranges and needn't reach their ends.
All inputs are finite; a program needn't handle non-finite values. No bound on the sum of `pinned` on one device may be relied on, other than what follows from the above.
Results may differ from the reference program's by a relative error of at most 0.0001.
Values sent between devices are 32-bit elements; how exact they have to be, the bound alone decides.
A program may use at most 128 MiB of HBM per device.

```python
import math
import jax
import jax.numpy as jnp

CYCLES = 2
SWEEPS = 4
NX = 16
NY = 2048
NZ = 128


def plant(entries, rng, smallest, high):
    longest = entries.shape.index(max(entries.shape))
    spots = []
    for shift in (0, 1):
        where = [jax.random.randint(jax.random.fold_in(rng, axis), (), 0, length) for axis, length in enumerate(entries.shape)]
        where[longest] = (where[longest] + shift) % entries.shape[longest]
        spots.append(tuple(where))
    return entries.at[spots[0]].set(smallest).at[spots[1]].set(high)


def level_of(own_key, shape, cuts, least, high):
    level, own = 1.0, jax.random.fold_in(own_key, 6)
    for axis_at, shards_of in cuts:
        draws = jnp.exp(jax.random.uniform(jax.random.fold_in(own, axis_at), (shards_of,), jnp.float32, least / len(cuts), high / len(cuts)))
        level = level * jnp.repeat(draws, shape[axis_at] // shards_of).reshape([-1 if axis == axis_at else 1 for axis in range(len(shape))])
    return level


def noise(rng, dims, width, bound, split=(), kind=jnp.bfloat16):
    entries = width * jax.random.normal(rng, dims, jnp.float32)
    if split:
        entries = entries * level_of(rng, dims, split, -0.22, 0.18)
    return jnp.clip(entries, -bound, bound).astype(kind)


def setup_inputs(seed: int = 0) -> dict:
    key_of = jax.random.split(jax.random.key(seed), 4)
    return {
        "stiffness": jnp.clip(jnp.exp(math.log(8.0) - 2.7725887 * jax.random.uniform(key_of[0], (NX, NY, NZ), jnp.float32) ** level_of(key_of[0], (NX, NY, NZ), ((0, 2), (1, 64)), -0.2, 0.2)), 0.5, 8.0),
        "prescribed": noise(key_of[1], (3, NX, NY, NZ), 1.0, 6.0, ((1, 2), (2, 64)), jnp.float32),
        "pinned": plant((jax.random.randint(key_of[2], (NX, NY, NZ), 0, 4) < 1).astype(jnp.int32), jax.random.fold_in(key_of[2], 1), 0, 1),
    }


relax_weight = 0.6
coarse_scale = 0.25
neighbour_offsets = [(step_x, step_y, step_z) for step_x in (-1, 0, 1) for step_y in (-1, 0, 1) for step_z in (-1, 0, 1) if (step_x, step_y, step_z) != (0, 0, 0)]


def pad_depth(array):
    return jnp.pad(array, [(0, 0)] * (array.ndim - 1) + [(1, 1)])


def pad_plane(array):
    return jnp.pad(array, [(0, 0)] * (array.ndim - 3) + [(1, 1), (1, 1), (0, 0)])


def shifted(array, step_x, step_y, step_z, extent_x, extent_y, extent_z):
    return array[..., 1 + step_x:1 + step_x + extent_x, 1 + step_y:1 + step_y + extent_y, 1 + step_z:1 + step_z + extent_z]


def op_diag(stiff_ext):
    extent_x = stiff_ext.shape[0] - 2
    extent_y = stiff_ext.shape[1] - 2
    extent_z = stiff_ext.shape[2]
    padded = pad_depth(stiff_ext)
    centre = stiff_ext[1:-1, 1:-1, :]
    summed = jnp.zeros_like(centre)
    for step_x, step_y, step_z in neighbour_offsets:
        weight = 0.5 ** (abs(step_x) + abs(step_y) + abs(step_z) - 1)
        summed = summed + weight * 0.5 * (centre + shifted(padded, step_x, step_y, step_z, extent_x, extent_y, extent_z))
    return summed


def apply_op(field_ext, stiff_ext):
    extent_x = field_ext.shape[1] - 2
    extent_y = field_ext.shape[2] - 2
    extent_z = field_ext.shape[3]
    field_pad = pad_depth(field_ext)
    stiff_pad = pad_depth(stiff_ext)
    centre_k = stiff_ext[1:-1, 1:-1, :]
    centre_u = field_ext[:, 1:-1, 1:-1, :]
    result = jnp.zeros_like(centre_u)
    for step_x, step_y, step_z in neighbour_offsets:
        weight = 0.5 ** (abs(step_x) + abs(step_y) + abs(step_z) - 1)
        coupling = weight * 0.5 * (centre_k + shifted(stiff_pad, step_x, step_y, step_z, extent_x, extent_y, extent_z))
        result = result + coupling * (centre_u - shifted(field_pad, step_x, step_y, step_z, extent_x, extent_y, extent_z))
    cross_parts = []
    for component in range(3):
        mixed_sum = jnp.zeros_like(centre_k)
        for partner_comp in range(3):
            if partner_comp == component:
                continue
            for sign_a in (-1, 1):
                for sign_b in (-1, 1):
                    offset = [0, 0, 0]
                    offset[component] = sign_a
                    offset[partner_comp] = sign_b
                    mixed_sum = mixed_sum + float(sign_a * sign_b) * shifted(field_pad[partner_comp], offset[0], offset[1], offset[2], extent_x, extent_y, extent_z)
        cross_parts.append(0.125 * centre_k * mixed_sum)
    return result - jnp.stack(cross_parts)


def restrict(array):
    lead = array.shape[:-3]
    size_x, size_y, size_z = array.shape[-3:]
    blocks = array.reshape(lead + (size_x // 2, 2, size_y // 2, 2, size_z // 2, 2))
    return jnp.sum(blocks, axis=(-5, -3, -1)) * 0.125


def prolong(array):
    return jnp.repeat(jnp.repeat(jnp.repeat(array, 2, axis=-3), 2, axis=-2), 2, axis=-1)


def reference(stiffness, prescribed, pinned):
    pinned_mask = pinned.astype(jnp.float32)
    free_mask = 1.0 - pinned_mask
    displace = prescribed * pinned_mask
    stiff_ext = pad_plane(stiffness)
    diagonal = op_diag(stiff_ext)
    coarse_ext = pad_plane(restrict(stiffness))
    coarse_diag = coarse_scale * op_diag(coarse_ext)
    for cycle_index in range(CYCLES):
        displace = displace - relax_weight * free_mask * apply_op(pad_plane(displace), stiff_ext) / diagonal
        residual = free_mask * (0.0 - apply_op(pad_plane(displace), stiff_ext))
        target = restrict(residual)
        correction = jnp.zeros_like(target)
        for sweep_index in range(SWEEPS):
            correction = correction + relax_weight * (target - coarse_scale * apply_op(pad_plane(correction), coarse_ext)) / coarse_diag
        displace = displace + free_mask * prolong(correction)
        displace = displace - relax_weight * free_mask * apply_op(pad_plane(displace), stiff_ext) / diagonal
    return displace
```

```python
import functools

import jax
import jax.numpy as jnp
from jax import lax
from jax.experimental import pallas as pl
from jax.experimental.pallas import tpu as pltpu
from jax.sharding import PartitionSpec as P

MESH = pl.DeviceIdType.MESH
PLANES = 13
ROWS = 72
COARSE_ROWS = 56
CHUNK = 2
BAND, OFF, DIAG_OFF, SIB, DIAG_SIB = range(5)
M_K, M_PIN, M_PR, M_KC, M_T, M_U, M_T2 = range(7)


def lane_iota():
    return lax.broadcasted_iota(jnp.int32, (1, 128), 1)


def roll(value, by):
    return pltpu.roll(value, by % 128, value.ndim - 1)


def z_pair(value, weights, step):
    low, high = weights
    return roll(value, step) * low, roll(value, -step) * high


def z_stage(field, scaled, zu, zv, dz, p, m, r0, n, weights, step):
    planes, rows = pl.ds(p, m), pl.ds(r0, n)
    for c in range(3):
        u = field[c, planes, rows]
        left, right = z_pair(u, weights, step)
        zu[c, planes, rows] = u + (left + right)
        dz[c, planes, rows] = 0.5 * (right - left)
    for c in range(3):
        v = scaled[c, planes, rows]
        left, right = z_pair(v, weights, step)
        zv[c, planes, rows] = v + (left + right)


def y_stage(field, zu, zv, dz, ep, em, ec, tv, p, m, r0, n):
    planes, mid, low, high = pl.ds(p, m), pl.ds(r0, n), pl.ds(r0 - 1, n), pl.ds(r0 + 1, n)
    for c in range(3):
        a = zu[c, planes, mid] + 0.5 * (zu[c, planes, low] + zu[c, planes, high])
        twice = a + a
        if c == 0:
            g = 0.25 * (field[1, planes, high] - field[1, planes, low]) + dz[2, planes, mid]
        elif c == 1:
            g = 0.25 * (field[0, planes, high] - field[0, planes, low])
            twice = twice + (dz[2, planes, high] - dz[2, planes, low])
        else:
            g = dz[0, planes, mid]
            twice = twice + (dz[1, planes, high] - dz[1, planes, low])
        ep[c, planes, mid] = a + g
        em[c, planes, mid] = a - g
        ec[c, planes, mid] = twice
        tv[c, planes, mid] = zv[c, planes, mid] + 0.5 * (zv[c, planes, low] + zv[c, planes, high])


def x_terms(field, k, g2, ep, em, ec, tv, c, p, m, rows):
    here, before, after = pl.ds(p, m), pl.ds(p - 1, m), pl.ds(p + 1, m)
    e = (ep[c, after, rows] + em[c, before, rows]) + ec[c, here, rows]
    mid = tv[c, here, rows]
    t = (tv[c, after, rows] + tv[c, before, rows]) + (mid + mid)
    return t + k * e - g2 * field[c, here, rows]


def kernel(
    bricks,
    stiff_in,
    pres_in,
    pin_in,
    out_hbm,
    k_own,
    k_f,
    pr_f,
    pin_f,
    g2_f,
    fh_f,
    free_f,
    fr8_f,
    ua,
    va,
    ub,
    vb,
    uc,
    ud,
    vd,
    ue,
    ve,
    res,
    out_f,
    zu,
    zv,
    dz,
    ep,
    em,
    ec,
    tv,
    prolonged,
    kc_b,
    kc_off,
    kc_sib,
    kt,
    t_b,
    t_off,
    t_sib,
    t2_b,
    t2_sib,
    tt,
    k_q,
    g_q,
    s_q,
    w_q,
    ca,
    cva,
    cb,
    cvb,
    czu,
    czv,
    cdz,
    cep,
    cem,
    cec,
    ctv,
    in_sem,
    send_sem,
    recv_sem,
):
    b = lax.axis_index("band")
    i = lax.axis_index("brick")
    c = lax.rem(i, 2)
    has_off = ((c == 0) & (i > 0)) | ((c == 1) & (i < bricks - 1))
    i_off = i - 1 + 2 * c
    i_sib = i + 1 - 2 * c
    own_row = pl.multiple_of(24 - 8 * c, 8)
    own_plane = 1 + 3 * b
    partners = {BAND: (1 - b, i), OFF: (b, i_off), DIAG_OFF: (1 - b, i_off), SIB: (b, i_sib), DIAG_SIB: (1 - b, i_sib)}

    locals_ = [
        pltpu.make_async_copy(stiff_in, k_f.at[pl.ds(own_plane, 8), pl.ds(own_row, 32)], in_sem.at[0]),
        pltpu.make_async_copy(pin_in, pin_f.at[pl.ds(own_plane, 8), pl.ds(own_row, 32)], in_sem.at[1]),
        pltpu.make_async_copy(pres_in, pr_f.at[:, pl.ds(own_plane, 8), pl.ds(own_row, 32)], in_sem.at[2]),
        pltpu.make_async_copy(stiff_in, k_own.at[:, pl.ds(own_row, 32)], in_sem.at[4]),
    ]
    for copy in locals_:
        copy.start()
    barrier = pltpu.get_barrier_semaphore()

    def greet(kind):
        pl.semaphore_signal(barrier, inc=1, device_id=partners[kind], device_id_type=MESH)

    for kind in (BAND, SIB, DIAG_SIB):
        greet(kind)

    @pl.when(has_off)
    def _():
        greet(OFF)
        greet(DIAG_OFF)

    @pl.when(jnp.logical_not(has_off))
    def _():
        deep = pl.ds(pl.multiple_of(8 + 40 * c, 8), 16)
        plain = jnp.zeros((PLANES, 16, 128), jnp.float32)
        k_f[:, deep] = plain
        pin_f[:, deep] = jnp.zeros((PLANES, 16, 128), jnp.int32)
        for comp in range(3):
            pr_f[comp, :, deep] = plain
            uc[comp, :, deep] = plain
        kc_off[...] = jnp.zeros(kc_off.shape, jnp.float32)
        t_off[...] = jnp.zeros(t_off.shape, jnp.float32)

    outer = 12 * b
    k_f[outer] = jnp.zeros((ROWS, 128), jnp.float32)
    for ref in (ep, em, tv):
        for comp in range(3):
            ref[comp, outer] = jnp.zeros((ROWS, 128), jnp.float32)
    edge = pl.ds(16, 24)
    for comp in range(3):
        for half in range(2):
            t_b[0, comp, half, edge] = jnp.zeros((24, 128), jnp.float32)
            t2_b[0, comp, half, edge] = jnp.zeros((24, 128), jnp.float32)
    for half in range(2):
        kc_b[0, half, edge] = jnp.zeros((24, 128), jnp.float32)

    lane = lane_iota()
    even = lax.rem(lane, 2) == 0
    fine_w = (jnp.where(lane == 0, 0.0, 0.5), jnp.where(lane == 127, 0.0, 0.5))
    coarse_w = (jnp.where(lane < 2, 0.0, 0.5), jnp.where(lane >= 126, 0.0, 0.5))
    first_core = lax.broadcasted_iota(jnp.int32, (8, 128), 0) * 0 + c == 0

    def by_core(zero, one):
        return jnp.where(first_core[: zero.shape[0]], zero, one)

    def halve(load, dst):
        sums = []
        for x in range(4):
            p = 2 * x
            top, low = pl.ds(16, 20, stride=2), pl.ds(17, 20, stride=2)
            sums.append((load(p, top) + load(p, low)) + (load(p + 1, top) + load(p + 1, low)))
        for half in range(2):
            first, second = sums[half], sums[half + 2]
            dst(half, jnp.where(even, first + roll(first, -1), second + roll(second, 1)))

    locals_[3].wait()

    def put_kc(half, value):
        kc_b[0, half, pl.ds(20, 20)] = 0.125 * value

    halve(lambda p, rows: k_own[p, rows], put_kc)

    copies = {}

    def prepare(message, kind, src, dst):
        copies[message, kind] = pltpu.make_async_remote_copy(
            src_ref=src,
            dst_ref=dst,
            send_sem=send_sem.at[message, kind],
            recv_sem=recv_sem.at[message, kind],
            device_id=partners[kind],
            device_id_type=MESH,
        )

    def fine_messages(message, src, dst, lead, src_plane, src_row, off_rows, depth):
        pick = (lambda ref, planes, rows: ref.at[:, planes, rows]) if lead else (lambda ref, planes, rows: ref.at[planes, rows])
        all_s, all_d = pl.ds(src_plane, 8), pl.ds(own_plane, 8)
        face_s = pl.ds(src_plane + (8 - depth) * (1 - b), depth)
        face_d = pl.ds((4 - depth) * (1 - b) + 9 * b, depth)
        rows_s = pl.ds(pl.multiple_of(src_row, 8), 32)
        off_s = pl.ds(pl.multiple_of(src_row + (32 - off_rows) * c, 8), off_rows)
        off_d = pl.ds(pl.multiple_of(48 * (1 - c) + (24 - off_rows) * c, 8), off_rows)
        sib_s = pl.ds(pl.multiple_of(src_row + 24 * (1 - c), 8), 8)
        sib_d = pl.ds(pl.multiple_of(8 + 48 * c, 8), 8)
        prepare(message, OFF, pick(src, all_s, off_s), pick(dst, all_d, off_d))
        prepare(message, DIAG_OFF, pick(src, face_s, off_s), pick(dst, face_d, off_d))
        prepare(message, BAND, pick(src, face_s, rows_s), pick(dst, face_d, pl.ds(own_row, 32)))
        prepare(message, SIB, pick(src, all_s, sib_s), pick(dst, all_d, sib_d))
        prepare(message, DIAG_SIB, pick(src, face_s, sib_s), pick(dst, face_d, sib_d))

    def coarse_messages(message, held, off, sib):
        lead = (slice(None),) * (len(held.shape) - 3)

        def rows(ref, slot, start, count):
            return ref.at[(slot, *lead, pl.ds(start, count))]

        sib_row = pl.multiple_of(24 - 8 * c, 8)
        prepare(message, OFF, rows(held, 0, 24, 16), off.at[0])
        prepare(message, DIAG_OFF, rows(held, 0, 24, 16), off.at[1])
        prepare(message, BAND, rows(held, 0, 16, 24), rows(held, 1, 16, 24))
        prepare(message, SIB, rows(held, 0, sib_row, 16), sib.at[0])
        prepare(message, DIAG_SIB, rows(held, 0, sib_row, 16), sib.at[1])

    fine_messages(M_PR, pres_in, pr_f, True, 0, 0, 8, 2)
    fine_messages(M_K, stiff_in, k_f, False, 0, 0, 16, 3)
    fine_messages(M_PIN, pin_in, pin_f, False, 0, 0, 16, 3)
    coarse_messages(M_KC, kc_b, kc_off, kc_sib)
    coarse_messages(M_T, t_b, t_off, t_sib)
    fine_messages(M_U, uc, uc, True, own_plane, own_row, 16, 3)
    block = pl.ds(pl.multiple_of(32 - 16 * c, 8), 8)
    prepare(M_T2, BAND, t2_b.at[0, :, :, pl.ds(16, 24)], t2_b.at[1, :, :, pl.ds(16, 24)])
    prepare(M_T2, SIB, t2_b.at[0, :, :, block], t2_sib.at[0])
    prepare(M_T2, DIAG_SIB, t2_b.at[0, :, :, block], t2_sib.at[1])

    def each(messages, act, off=True):
        if off:

            @pl.when(has_off)
            def _():
                for kind in (OFF, DIAG_OFF):
                    for message in messages:
                        act(copies[message, kind])

        for kind in (BAND, DIAG_SIB, SIB):
            for message in messages:
                act(copies[message, kind])

    def start(*messages, off=True):
        each(messages, lambda copy: copy.start(), off)

    def received(*messages, off=True):
        each(messages, lambda copy: copy.wait_recv(), off)

    def sent(*messages, off=True):
        each(messages, lambda copy: copy.wait_send(), off)

    pl.semaphore_wait(barrier, 3 + 2 * has_off.astype(jnp.int32))
    start(M_PR, M_K, M_PIN)
    start(M_KC)

    locals_[0].wait()
    locals_[1].wait()
    locals_[2].wait()
    received(M_PR, M_K, M_PIN)

    def begin(p, m, r0, n):
        planes, rows = pl.ds(p, m), pl.ds(r0, n)
        pinned = pin_f[planes, rows].astype(jnp.float32)
        k = k_f[planes, rows]
        for comp in range(3):
            u = pr_f[comp, planes, rows] * pinned
            ua[comp, planes, rows] = u
            va[comp, planes, rows] = k * u

    for q in range(0, 10, CHUNK):
        begin(1 + b + q, CHUNK, 14, 44)

    for p in range(1, 12):
        k = k_f[p, pl.ds(13, 46)]
        left, right = z_pair(k, fine_w, 1)
        zu[0, p, pl.ds(13, 46)] = k + (left + right)
    for p in range(1, 12):
        tv[0, p, pl.ds(14, 44)] = zu[0, p, pl.ds(14, 44)] + 0.5 * (zu[0, p, pl.ds(13, 44)] + zu[0, p, pl.ds(15, 44)])
    for p in range(1, 12):
        free = 1.0 - pin_f[p, pl.ds(13, 46)].astype(jnp.float32)
        free_f[p, pl.ds(13, 46)] = free
        fr8_f[p, pl.ds(13, 46)] = 0.0625 * free
    for q in range(10):
        p, rows = 1 + b + q, pl.ds(14, 44)
        k = k_f[p, rows]
        t = tv[0, p, rows] + 0.5 * (tv[0, p - 1, rows] + tv[0, p + 1, rows])
        g2_f[p, rows] = 16.0 * k + 2.0 * t
        diagonal = 6.0 * k + t
        fh_f[p, rows] = jnp.where(k > 0.0, 0.3 * free_f[p, rows] / jnp.where(k > 0.0, diagonal, 1.0), 0.0)

    def fine(field, scaled, p, m, out_p, out_m, r0, n, emit):
        for q in range(0, m, CHUNK):
            size = min(CHUNK, m - q)
            z_stage(field, scaled, zu, zv, dz, p + q, size, r0 - 1, n + 2, fine_w, 1)
            y_stage(field, zu, zv, dz, ep, em, ec, tv, p + q, size, r0, n)
        rows = pl.ds(r0, n)
        for done in range(0, out_m, CHUNK):
            size = min(CHUNK, out_m - done)
            at = out_p + done
            here = pl.ds(at, size)
            k, g2 = k_f[here, rows], g2_f[here, rows]
            for comp in range(3):
                emit(comp, here, rows, k, field, x_terms(field, k, g2, ep, em, ec, tv, comp, at, size, rows))

    def sweep_to(out_u, out_v):
        def emit(comp, here, rows, k, field, terms):
            u = field[comp, here, rows] + fh_f[here, rows] * terms
            out_u[comp, here, rows] = u
            if out_v is not None:
                out_v[comp, here, rows] = u * k

        return emit

    def to_residual(comp, here, rows, k, field, terms):
        res[comp, here, rows] = fr8_f[here, rows] * terms

    def sweep_wide(field, scaled, out_u, out_v):
        fine(field, scaled, 1, 11, 1 + b, 10, 14, 44, sweep_to(out_u, out_v))

    def sweep_near(field, scaled, out_u, out_v):
        fine(field, scaled, 1 + b, 10, 1 + 2 * b, 9, 15, 42, sweep_to(out_u, out_v))

    def residual(field, scaled):
        fine(field, scaled, 1 + 2 * b, 9, own_plane, 8, 16, 40, to_residual)

    sweep_near(ua, va, ub, vb)
    own = (pl.ds(own_plane, 8), pl.ds(own_row, 32))
    for comp in range(3):
        uc[(comp, *own)] = ub[(comp, *own)]
    residual(ub, vb)

    def put_target(dst):
        for comp in range(3):

            def put(half, value, comp=comp):
                dst[0, comp, half, pl.ds(20, 20)] = value

            halve(lambda p, rows, comp=comp: res[comp, own_plane + p, rows], put)

    put_target(t_b)
    start(M_T)
    start(M_U)

    def assemble(held, off, sib, dst):
        dst[pl.ds(24, 12)] = held[pl.ds(24, 12)]
        dst[pl.ds(14, 6)] = by_core(off[pl.ds(2, 6)], sib[pl.ds(10, 6)])
        dst[pl.ds(20, 4)] = by_core(off[pl.ds(8, 4)], held[pl.ds(20, 4)])
        dst[pl.ds(36, 4)] = by_core(held[pl.ds(36, 4)], off[pl.ds(0, 4)])
        dst[pl.ds(40, 6)] = by_core(sib[pl.ds(4, 6)], off[pl.ds(4, 6)])

    def repack(load, rows, emit):
        for half in range(2):
            low, high = load(b, half, rows), load(1 - b, half, rows)
            emit(1 + half, jnp.where(even, low, roll(high, 1)))
            emit(3 + half, jnp.where(even, roll(low, -1), high))

    received(M_KC)
    for slot in range(2):
        for half in range(2):
            assemble(kc_b.at[slot, half], kc_off.at[slot, half], kc_sib.at[slot, half], kt.at[slot, half])

    def put_kq(q, value):
        k_q[q, pl.ds(14, 32)] = value

    repack(lambda slot, half, rows: kt[slot, half, rows], pl.ds(14, 32), put_kq)

    def wrap_after(value):
        return jnp.where(even, roll(value, -1), 0.0)

    def wrap_before(value):
        return jnp.where(even, 0.0, roll(value, 1))

    for q in range(1, 5):
        k = k_q[q, pl.ds(14, 32)]
        left, right = z_pair(k, coarse_w, 2)
        czu[0, q, pl.ds(14, 32)] = k + (left + right)
    whole = pl.ds(15, 30)
    for q in range(1, 5):
        ctv[0, q, whole] = czu[0, q, whole] + 0.5 * (czu[0, q, pl.ds(14, 30)] + czu[0, q, pl.ds(16, 30)])
    ctv[0, 5, whole] = wrap_after(ctv[0, 1, whole])
    ctv[0, 0, whole] = wrap_before(ctv[0, 4, whole])
    for q in range(1, 5):
        k = k_q[q, whole]
        t = ctv[0, q, whole] + 0.5 * (ctv[0, q - 1, whole] + ctv[0, q + 1, whole])
        g_q[q, whole] = 16.0 * k + 2.0 * t
        s_q[q, whole] = jnp.where(k > 0.0, 0.3 / jnp.where(k > 0.0, 6.0 * k + t, 1.0), 0.0)

    def coarse_sweep(field, scaled, out_u, out_v, r0, n):
        z_stage(field, scaled, czu, czv, cdz, 1, 4, r0 - 1, n + 2, coarse_w, 2)
        y_stage(field, czu, czv, cdz, cep, cem, cec, ctv, 1, 4, r0, n)
        rows = pl.ds(r0, n)
        for comp in range(3):
            cep[comp, 5, rows] = wrap_after(cep[comp, 1, rows])
            cem[comp, 0, rows] = wrap_before(cem[comp, 4, rows])
            ctv[comp, 5, rows] = wrap_after(ctv[comp, 1, rows])
            ctv[comp, 0, rows] = wrap_before(ctv[comp, 4, rows])
        here = pl.ds(1, 4)
        k, g2, s = k_q[here, rows], g_q[here, rows], s_q[here, rows]
        for comp in range(3):
            terms = x_terms(field, k, g2, cep, cem, cec, ctv, comp, 1, 4, rows)
            u = field[comp, here, rows] + (w_q[comp, here, rows] + s * terms)
            out_u[comp, here, rows] = u
            if out_v is not None:
                out_v[comp, here, rows] = u * k

    def coarse(load, r0, n):
        rows = pl.ds(r0, n)
        for comp in range(3):

            def put(q, value, comp=comp):
                w = 8.0 * s_q[q, rows] * value
                w_q[comp, q, rows] = w
                ca[comp, q, rows] = w
                cva[comp, q, rows] = w * k_q[q, rows]

            repack(lambda slot, half, at, comp=comp: load(slot, comp, half, at), rows, put)
        coarse_sweep(ca, cva, cb, cvb, r0 + 1, n - 2)
        coarse_sweep(cb, cvb, ca, cva, r0 + 2, n - 4)
        coarse_sweep(ca, cva, cb, None, r0 + 3, n - 6)
        last, count = r0 + 3, n - 6
        for comp in range(3):
            for q in range(1, 5):
                value = cb[comp, q, pl.ds(last, count)]
                for x, part in ((q - 1, jnp.where(even, value, roll(value, 1))), (q + 3, jnp.where(even, roll(value, -1), value))):
                    prolonged[comp, x, pl.ds(2 * last - 24, count, stride=2)] = part
                    prolonged[comp, x, pl.ds(2 * last - 23, count, stride=2)] = part

    def correct(field, out_u, out_v, p, m, r0, n):
        rows = pl.ds(r0, n)
        for q in range(m):
            at = p + q
            x = (at - 1 + 5 * b) // 2
            k, free = k_f[at, rows], free_f[at, rows]
            for comp in range(3):
                u = field[comp, at, rows] + free * prolonged[comp, x, rows]
                out_u[comp, at, rows] = u
                out_v[comp, at, rows] = u * k

    received(M_T)
    for slot in range(2):
        for comp in range(3):
            for half in range(2):
                assemble(
                    t_b.at[slot, comp, half], t_off.at[slot, comp, half], t_sib.at[slot, comp, half], tt.at[slot, comp, half]
                )
    coarse(lambda slot, comp, half, rows: tt[slot, comp, half, rows], 15, 30)
    received(M_U)
    correct(uc, ud, vd, 1, 11, 13, 46)
    sweep_wide(ud, vd, ue, ve)

    sweep_near(ue, ve, ud, vd)
    residual(ud, vd)
    put_target(t2_b)
    start(M_T2, off=False)
    received(M_T2, off=False)
    for slot in range(2):
        for comp in range(3):
            for half in range(2):
                tt[slot, comp, half, pl.ds(16, 24)] = t2_b[slot, comp, half, pl.ds(16, 24)]
                near = t2_sib[slot, comp, half, pl.ds(4, 4)]
                tt[slot, comp, half, pl.ds(16, 4)] = near
                tt[slot, comp, half, pl.ds(40, 4)] = near
    coarse(lambda slot, comp, half, rows: tt[slot, comp, half, rows], 16, 28)
    correct(ud, ue, ve, 1 + 2 * b, 9, 15, 42)
    fine(ue, ve, 1 + 2 * b, 9, own_plane, 8, 16, 40, sweep_to(out_f, None))
    result = pltpu.make_async_copy(out_f.at[(slice(None), *own)], out_hbm, in_sem.at[3])
    result.start()
    sent(M_PR, M_K, M_PIN, M_KC, M_T, M_U)
    sent(M_T2, off=False)
    result.wait()


def solution(mesh):
    bricks = mesh.shape["brick"]

    def body(stiffness, prescribed, pinned):
        def f32(*shape):
            return pltpu.VMEM(shape, jnp.float32)

        one, three = f32(PLANES, ROWS, 128), f32(3, PLANES, ROWS, 128)
        q1, q3 = f32(6, COARSE_ROWS, 128), f32(3, 6, COARSE_ROWS, 128)
        scratch = [
            f32(8, ROWS, 128),
            one,
            three,
            pltpu.VMEM((PLANES, ROWS, 128), jnp.int32),
            *[one] * 4,
            *[three] * 11,
            *[three] * 7,
            f32(3, 8, ROWS, 128),
            f32(2, 2, COARSE_ROWS, 128),
            f32(2, 2, 16, 128),
            f32(2, 2, 16, 128),
            f32(2, 2, COARSE_ROWS, 128),
            f32(2, 3, 2, COARSE_ROWS, 128),
            f32(2, 3, 2, 16, 128),
            f32(2, 3, 2, 16, 128),
            f32(2, 3, 2, COARSE_ROWS, 128),
            f32(2, 3, 2, 8, 128),
            f32(2, 3, 2, COARSE_ROWS, 128),
            *[q1] * 3,
            *[q3] * 5,
            *[q3] * 7,
            pltpu.SemaphoreType.DMA((5,)),
            pltpu.SemaphoreType.DMA((7, 5)),
            pltpu.SemaphoreType.DMA((7, 5)),
        ]
        hbm = pl.BlockSpec(memory_space=pl.ANY)
        return pl.pallas_call(
            functools.partial(kernel, bricks),
            out_shape=jax.ShapeDtypeStruct(prescribed.shape, jnp.float32),
            in_specs=[hbm] * 3,
            out_specs=hbm,
            scratch_shapes=scratch,
            compiler_params=pltpu.CompilerParams(collective_id=0, has_side_effects=True, vmem_limit_bytes=58 * 2**20),
        )(stiffness, prescribed, pinned)

    return jax.shard_map(
        body,
        mesh=mesh,
        in_specs=(P("band", "brick", None), P(None, "band", "brick", None), P("band", "brick", None)),
        out_specs=P(None, "band", "brick", None),
        check_vma=False,
    )
```

```python
import functools

import jax
import jax.numpy as jnp
from jax import lax
from jax.experimental import pallas as pl
from jax.experimental.pallas import tpu as pltpu
from jax.sharding import PartitionSpec as P

MESH = pl.DeviceIdType.MESH
PLANES = 13
ROWS = 48
COARSE_ROWS = 32
CHUNK = 2
BAND, UP, DOWN, DIAG_UP, DIAG_DOWN = range(5)
MESSAGES = 8
M_IN, M_FACE_U, M_FACE_K, M_FACE_FREE, M_KC, M_T, M_U, M_T2 = range(MESSAGES)


def lane_iota():
    return lax.broadcasted_iota(jnp.int32, (1, 128), 1)


def roll(value, by):
    return pltpu.roll(value, by % 128, value.ndim - 1)


def z_pair(value, weights, step):
    low, high = weights
    return roll(value, step) * low, roll(value, -step) * high


def z_stage(field, scaled, zu, zv, dz, p, m, r0, n, weights, step):
    planes, rows = pl.ds(p, m), pl.ds(r0, n)
    for c in range(3):
        u = field[c, planes, rows]
        left, right = z_pair(u, weights, step)
        zu[c, planes, rows] = u + (left + right)
        dz[c, planes, rows] = 0.5 * (right - left)
    for c in range(3):
        v = scaled[c, planes, rows]
        left, right = z_pair(v, weights, step)
        zv[c, planes, rows] = v + (left + right)


def y_stage(field, zu, zv, dz, ep, em, ec, tv, p, m, r0, n):
    planes, mid, low, high = pl.ds(p, m), pl.ds(r0, n), pl.ds(r0 - 1, n), pl.ds(r0 + 1, n)
    for c in range(3):
        a = zu[c, planes, mid] + 0.5 * (zu[c, planes, low] + zu[c, planes, high])
        twice = a + a
        if c == 0:
            g = 0.25 * (field[1, planes, high] - field[1, planes, low]) + dz[2, planes, mid]
        elif c == 1:
            g = 0.25 * (field[0, planes, high] - field[0, planes, low])
            twice = twice + (dz[2, planes, high] - dz[2, planes, low])
        else:
            g = dz[0, planes, mid]
            twice = twice + (dz[1, planes, high] - dz[1, planes, low])
        ep[c, planes, mid] = a + g
        em[c, planes, mid] = a - g
        ec[c, planes, mid] = twice
        tv[c, planes, mid] = zv[c, planes, mid] + 0.5 * (zv[c, planes, low] + zv[c, planes, high])


def x_terms(field, k, g2, ep, em, ec, tv, c, p, m, rows):
    here, before, after = pl.ds(p, m), pl.ds(p - 1, m), pl.ds(p + 1, m)
    e = (ep[c, after, rows] + em[c, before, rows]) + ec[c, here, rows]
    mid = tv[c, here, rows]
    t = (tv[c, after, rows] + tv[c, before, rows]) + (mid + mid)
    return t + k * e - g2 * field[c, here, rows]


def kernel(
    bricks,
    stiff_in,
    pres_in,
    pin_in,
    out_hbm,
    pr_in,
    pin_own,
    k_own,
    k_f,
    free_f,
    fr8_f,
    g2_f,
    fh_f,
    ua,
    va,
    ub,
    vb,
    uc,
    ud,
    vd,
    ue,
    ve,
    res,
    out_f,
    zu,
    zv,
    dz,
    ep,
    em,
    ec,
    tv,
    prolonged,
    in_pack,
    in_land,
    in_diag_pack,
    in_diag_land,
    u_pack,
    u_land,
    u_diag_pack,
    u_diag_land,
    kc,
    t_1,
    t_2,
    k_q,
    g_q,
    s_q,
    w_q,
    ca,
    cva,
    cb,
    cvb,
    czu,
    czv,
    cdz,
    cep,
    cem,
    cec,
    ctv,
    in_sem,
    send_sem,
    recv_sem,
):
    b = lax.axis_index("band")
    i = lax.axis_index("brick")
    has_up, has_down = i > 0, i < bricks - 1
    own_plane = 1 + 3 * b
    planes_own = pl.ds(own_plane, 8)
    partners = {BAND: (1 - b, i), UP: (b, i - 1), DOWN: (b, i + 1), DIAG_UP: (1 - b, i - 1), DIAG_DOWN: (1 - b, i + 1)}

    locals_ = [
        pltpu.make_async_copy(stiff_in, k_own, in_sem.at[0]),
        pltpu.make_async_copy(pin_in, pin_own, in_sem.at[1]),
        pltpu.make_async_copy(pres_in, pr_in, in_sem.at[2]),
    ]
    for copy in locals_:
        copy.start()
    barrier = pltpu.get_barrier_semaphore()

    def greet(kind):
        pl.semaphore_signal(barrier, inc=1, device_id=partners[kind], device_id_type=MESH)

    greet(BAND)

    @pl.when(has_up)
    def _():
        greet(UP)
        greet(DIAG_UP)

    @pl.when(has_down)
    def _():
        greet(DOWN)
        greet(DIAG_DOWN)

    def outside(slot, rows):
        for ref in (in_land, in_diag_land, u_land, u_diag_land):
            ref[slot] = jnp.zeros(ref.shape[1:], jnp.float32)
        for band in range(2):
            for half in range(2):
                kc[band, half, rows] = jnp.zeros((8, 128), jnp.float32)
                for comp in range(3):
                    t_1[band, comp, half, rows] = jnp.zeros((8, 128), jnp.float32)
                    t_2[band, comp, half, rows] = jnp.zeros((8, 128), jnp.float32)

    @pl.when(jnp.logical_not(has_up))
    def _():
        outside(1, pl.ds(0, 8))

    @pl.when(jnp.logical_not(has_down))
    def _():
        outside(0, pl.ds(24, 8))

    outer = 12 * b
    k_f[outer] = jnp.zeros((ROWS, 128), jnp.float32)
    for ref in (ep, em, tv):
        for comp in range(3):
            ref[comp, outer] = jnp.zeros((ROWS, 128), jnp.float32)

    lane = lane_iota()
    even = lax.rem(lane, 2) == 0
    fine_w = (jnp.where(lane == 0, 0.0, 0.5), jnp.where(lane == 127, 0.0, 0.5))
    coarse_w = (jnp.where(lane < 2, 0.0, 0.5), jnp.where(lane >= 126, 0.0, 0.5))

    def halve(load, first_row, emit):
        sums = []
        for x in range(4):
            p = 2 * x
            top, low = pl.ds(first_row, 16, stride=2), pl.ds(first_row + 1, 16, stride=2)
            sums.append((load(p, top) + load(p, low)) + (load(p + 1, top) + load(p + 1, low)))
        for half in range(2):
            first, second = sums[half], sums[half + 2]
            emit(half, jnp.where(even, first + roll(first, -1), second + roll(second, 1)))

    copies = {}

    def prepare(message, kind, src, dst):
        copies[message, kind] = pltpu.make_async_remote_copy(
            src_ref=src,
            dst_ref=dst,
            send_sem=send_sem.at[message, kind],
            recv_sem=recv_sem.at[message, kind],
            device_id=partners[kind],
            device_id_type=MESH,
        )

    def face_message(message, ref, depth, lead):
        src, dst = pl.ds(4 + (5 - depth) * (1 - b), depth), pl.ds((4 - depth) * (1 - b) + 9 * b, depth)
        rows = pl.ds(8, 32)
        if lead:
            prepare(message, BAND, ref.at[:, src, rows], ref.at[:, dst, rows])
        else:
            prepare(message, BAND, ref.at[src, rows], ref.at[dst, rows])

    def packed_messages(message, pack, land, diag_pack, diag_land):
        for slot, near, far in ((0, UP, DIAG_UP), (1, DOWN, DIAG_DOWN)):
            prepare(message, near, pack.at[slot], land.at[slot])
            prepare(message, far, diag_pack.at[slot], diag_land.at[slot])

    def coarse_messages(message, ref):
        def at(band, start, count):
            if len(ref.shape) == 4:
                return ref.at[band, :, pl.ds(start, count)]
            return ref.at[band, :, :, pl.ds(start, count)]

        prepare(message, BAND, at(0, 8, 16), at(1, 8, 16))
        prepare(message, UP, at(0, 8, 8), at(0, 24, 8))
        prepare(message, DIAG_UP, at(0, 8, 8), at(1, 24, 8))
        prepare(message, DOWN, at(0, 16, 8), at(0, 0, 8))
        prepare(message, DIAG_DOWN, at(0, 16, 8), at(1, 0, 8))

    packed_messages(M_IN, in_pack, in_land, in_diag_pack, in_diag_land)
    face_message(M_FACE_U, ua, 2, True)
    face_message(M_FACE_K, k_f, 3, False)
    face_message(M_FACE_FREE, free_f, 3, False)
    coarse_messages(M_KC, kc)
    coarse_messages(M_T, t_1)
    coarse_messages(M_T2, t_2)
    packed_messages(M_U, u_pack, u_land, u_diag_pack, u_diag_land)
    face_message(M_U, uc, 3, True)

    def each(messages, act, above, below):
        for holds, kinds in ((above, (UP, DIAG_UP)), (below, (DOWN, DIAG_DOWN))):
            found = [copies[m, kind] for m in messages for kind in kinds if (m, kind) in copies]
            if found:

                @pl.when(holds)
                def _(found=found):
                    for copy in found:
                        act(copy)

        for m in messages:
            if (m, BAND) in copies:
                act(copies[m, BAND])

    def start(*messages):
        each(messages, lambda copy: copy.start(), has_up, has_down)

    def received(*messages):
        each(messages, lambda copy: copy.wait_recv(), has_down, has_up)

    def sent(*messages):
        each(messages, lambda copy: copy.wait_send(), has_up, has_down)

    def edges(slot, depth):
        return (pl.ds(8, depth), pl.ds(40, depth)) if slot == 0 else (pl.ds(40 - depth, depth), pl.ds(8 - depth, depth))

    def pack(fields, dst, diag_dst):
        total = sum(depth for _, depth in fields)
        face = own_plane + 5 * (1 - b)
        for slot in range(2):
            at = 0
            for load, depth in fields:
                rows = edges(slot, depth)[0]
                for q in range(8):
                    dst[slot, pl.ds(q * total + at, depth)] = load(own_plane + q, rows)
                for q in range(3):
                    diag_dst[slot, pl.ds(q * total + at, depth)] = load(face + q, rows)
                at += depth

    def unpack(fields, land, diag_land):
        total = sum(depth for _, depth in fields)
        face = 1 + 8 * (1 - b)
        for slot in range(2):
            at = 0
            for store, depth in fields:
                rows = edges(slot, depth)[1]
                for q in range(8):
                    store(own_plane + q, rows, land[slot, pl.ds(q * total + at, depth)])
                for q in range(3):
                    store(face + q, rows, diag_land[slot, pl.ds(q * total + at, depth)])
                at += depth

    def load_of(ref, comp=None):
        return (lambda p, rows: ref[p, rows]) if comp is None else (lambda p, rows: ref[comp, p, rows])

    def store_of(ref, comp=None):
        def store(p, rows, value):
            if comp is None:
                ref[p, rows] = value
            else:
                ref[comp, p, rows] = value

        return store

    for copy in locals_:
        copy.wait()
    own_rows = pl.ds(8, 32)
    for q in range(8):
        at = own_plane + q
        pinned = pin_own[q].astype(jnp.float32)
        free_f[at, own_rows] = 1.0 - pinned
        k = k_own[q]
        k_f[at, own_rows] = k
        for comp in range(3):
            u = pr_in[comp, q] * pinned
            ua[comp, at, own_rows] = u
            va[comp, at, own_rows] = k * u
    pack(
        [(load_of(ua, 0), 2), (load_of(ua, 1), 2), (load_of(ua, 2), 2), (load_of(k_f), 3), (load_of(free_f), 3)],
        in_pack,
        in_diag_pack,
    )

    def put_kc(half, value):
        kc[0, half, pl.ds(8, 16)] = 0.125 * value

    halve(lambda p, rows: k_own[p, rows], 0, put_kc)

    pl.semaphore_wait(barrier, 1 + 2 * has_up.astype(jnp.int32) + 2 * has_down.astype(jnp.int32))
    start(M_IN, M_FACE_U, M_FACE_K, M_FACE_FREE)
    start(M_KC)
    received(M_IN, M_FACE_U, M_FACE_K, M_FACE_FREE)
    unpack(
        [(store_of(ua, 0), 2), (store_of(ua, 1), 2), (store_of(ua, 2), 2), (store_of(k_f), 3), (store_of(free_f), 3)],
        in_land,
        in_diag_land,
    )
    near = pl.ds(6, 36)
    for q in range(10):
        at = 1 + b + q
        k = k_f[at, near]
        for comp in range(3):
            va[comp, at, near] = k * ua[comp, at, near]

    for p in range(1, 12):
        k = k_f[p, pl.ds(5, 38)]
        left, right = z_pair(k, fine_w, 1)
        zu[0, p, pl.ds(5, 38)] = k + (left + right)
        fr8_f[p, own_rows] = 0.0625 * free_f[p, own_rows]
    for p in range(1, 12):
        tv[0, p, near] = zu[0, p, near] + 0.5 * (zu[0, p, pl.ds(5, 36)] + zu[0, p, pl.ds(7, 36)])
    for q in range(10):
        p = 1 + b + q
        k = k_f[p, near]
        t = tv[0, p, near] + 0.5 * (tv[0, p - 1, near] + tv[0, p + 1, near])
        g2_f[p, near] = 16.0 * k + 2.0 * t
        diagonal = 6.0 * k + t
        fh_f[p, near] = jnp.where(k > 0.0, 0.3 * free_f[p, near] / jnp.where(k > 0.0, diagonal, 1.0), 0.0)

    def fine(field, scaled, p, m, out_p, out_m, r0, n, emit):
        rows = pl.ds(r0, n)
        done = 0
        for q in range(0, m, CHUNK):
            size = min(CHUNK, m - q)
            z_stage(field, scaled, zu, zv, dz, p + q, size, r0 - 1, n + 2, fine_w, 1)
            y_stage(field, zu, zv, dz, ep, em, ec, tv, p + q, size, r0, n)
            while done < out_m:
                out_size = min(CHUNK, out_m - done)
                if q + size < min(m, done + out_size + 2):
                    break
                at = out_p + done
                here = pl.ds(at, out_size)
                k, g2 = k_f[here, rows], g2_f[here, rows]
                for comp in range(3):
                    emit(comp, here, rows, k, field, x_terms(field, k, g2, ep, em, ec, tv, comp, at, out_size, rows))
                done += out_size

    def sweep_to(out_u, out_v):
        def emit(comp, here, rows, k, field, terms):
            u = field[comp, here, rows] + fh_f[here, rows] * terms
            out_u[comp, here, rows] = u
            if out_v is not None:
                out_v[comp, here, rows] = u * k

        return emit

    def to_residual(comp, here, rows, k, field, terms):
        res[comp, here, rows] = fr8_f[here, rows] * terms

    def sweep_wide(field, scaled, out_u, out_v):
        fine(field, scaled, 1, 11, 1 + b, 10, 6, 36, sweep_to(out_u, out_v))

    def sweep_near(field, scaled, out_u, out_v):
        fine(field, scaled, 1 + b, 10, 1 + 2 * b, 9, 7, 34, sweep_to(out_u, out_v))

    def residual(field, scaled):
        fine(field, scaled, 1 + 2 * b, 9, own_plane, 8, 8, 32, to_residual)

    def put_target(dst):
        for comp in range(3):

            def put(half, value, comp=comp):
                dst[0, comp, half, pl.ds(8, 16)] = value

            halve(lambda p, rows, comp=comp: res[comp, own_plane + p, rows], 8, put)

    sweep_near(ua, va, ub, vb)
    residual(ub, vb)
    put_target(t_1)
    start(M_T)
    for comp in range(3):
        uc[comp, planes_own, own_rows] = ub[comp, planes_own, own_rows]
    u_fields = [(load_of(ub, 0), 3), (load_of(ub, 1), 3), (load_of(ub, 2), 3)]
    pack(u_fields, u_pack, u_diag_pack)
    start(M_U)

    def repack(load, rows, emit):
        for half in range(2):
            low, high = load(b, half, rows), load(1 - b, half, rows)
            emit(1 + half, jnp.where(even, low, roll(high, 1)))
            emit(3 + half, jnp.where(even, roll(low, -1), high))

    def wrap_after(value):
        return jnp.where(even, roll(value, -1), 0.0)

    def wrap_before(value):
        return jnp.where(even, 0.0, roll(value, 1))

    received(M_KC)

    def put_kq(q, value):
        k_q[q, pl.ds(2, 28)] = value

    repack(lambda slot, half, rows: kc[slot, half, rows], pl.ds(2, 28), put_kq)
    for q in range(1, 5):
        k = k_q[q, pl.ds(2, 28)]
        left, right = z_pair(k, coarse_w, 2)
        czu[0, q, pl.ds(2, 28)] = k + (left + right)
    whole = pl.ds(3, 26)
    for q in range(1, 5):
        ctv[0, q, whole] = czu[0, q, whole] + 0.5 * (czu[0, q, pl.ds(2, 26)] + czu[0, q, pl.ds(4, 26)])
    ctv[0, 5, whole] = wrap_after(ctv[0, 1, whole])
    ctv[0, 0, whole] = wrap_before(ctv[0, 4, whole])
    for q in range(1, 5):
        k = k_q[q, whole]
        t = ctv[0, q, whole] + 0.5 * (ctv[0, q - 1, whole] + ctv[0, q + 1, whole])
        g_q[q, whole] = 16.0 * k + 2.0 * t
        s_q[q, whole] = jnp.where(k > 0.0, 0.3 / jnp.where(k > 0.0, 6.0 * k + t, 1.0), 0.0)

    def coarse_sweep(field, scaled, out_u, out_v, r0, n):
        z_stage(field, scaled, czu, czv, cdz, 1, 4, r0 - 1, n + 2, coarse_w, 2)
        y_stage(field, czu, czv, cdz, cep, cem, cec, ctv, 1, 4, r0, n)
        rows = pl.ds(r0, n)
        for comp in range(3):
            cep[comp, 5, rows] = wrap_after(cep[comp, 1, rows])
            cem[comp, 0, rows] = wrap_before(cem[comp, 4, rows])
            ctv[comp, 5, rows] = wrap_after(ctv[comp, 1, rows])
            ctv[comp, 0, rows] = wrap_before(ctv[comp, 4, rows])
        here = pl.ds(1, 4)
        k, g2, s = k_q[here, rows], g_q[here, rows], s_q[here, rows]
        for comp in range(3):
            terms = x_terms(field, k, g2, cep, cem, cec, ctv, comp, 1, 4, rows)
            u = field[comp, here, rows] + (w_q[comp, here, rows] + s * terms)
            out_u[comp, here, rows] = u
            if out_v is not None:
                out_v[comp, here, rows] = u * k

    def coarse(target, r0, n):
        rows = pl.ds(r0, n)
        for comp in range(3):

            def put(q, value, comp=comp):
                w = 8.0 * s_q[q, rows] * value
                w_q[comp, q, rows] = w
                ca[comp, q, rows] = w
                cva[comp, q, rows] = w * k_q[q, rows]

            repack(lambda slot, half, at, comp=comp: target[slot, comp, half, at], rows, put)
        coarse_sweep(ca, cva, cb, cvb, r0 + 1, n - 2)
        coarse_sweep(cb, cvb, ca, cva, r0 + 2, n - 4)
        coarse_sweep(ca, cva, cb, None, r0 + 3, n - 6)
        last, count = r0 + 3, n - 6
        for comp in range(3):
            for q in range(1, 5):
                value = cb[comp, q, pl.ds(last, count)]
                for x, part in ((q - 1, jnp.where(even, value, roll(value, 1))), (q + 3, jnp.where(even, roll(value, -1), value))):
                    prolonged[comp, x, pl.ds(2 * last - 8, count, stride=2)] = part
                    prolonged[comp, x, pl.ds(2 * last - 7, count, stride=2)] = part

    def correct(field, out_u, out_v, p, m, r0, n):
        rows = pl.ds(r0, n)
        for q in range(m):
            at = p + q
            x = (at - 1 + 5 * b) // 2
            k, free = k_f[at, rows], free_f[at, rows]
            for comp in range(3):
                u = field[comp, at, rows] + free * prolonged[comp, x, rows]
                out_u[comp, at, rows] = u
                out_v[comp, at, rows] = u * k

    received(M_T)
    coarse(t_1, 3, 26)
    received(M_U)
    unpack([(store_of(uc, 0), 3), (store_of(uc, 1), 3), (store_of(uc, 2), 3)], u_land, u_diag_land)
    correct(uc, ud, vd, 1, 11, 5, 38)
    sweep_wide(ud, vd, ue, ve)

    sweep_near(ue, ve, ud, vd)
    residual(ud, vd)
    put_target(t_2)
    start(M_T2)
    received(M_T2)
    coarse(t_2, 4, 24)
    correct(ud, ue, ve, 1 + 2 * b, 9, 7, 34)
    fine(ue, ve, 1 + 2 * b, 9, own_plane, 8, 8, 32, sweep_to(out_f, None))
    result = pltpu.make_async_copy(out_f.at[:, planes_own, own_rows], out_hbm, in_sem.at[3])
    result.start()
    sent(M_IN, M_FACE_U, M_FACE_K, M_FACE_FREE, M_KC, M_T, M_U, M_T2)
    result.wait()


def solution(mesh):
    bricks = mesh.shape["brick"]

    def body(stiffness, prescribed, pinned):
        def f32(*shape):
            return pltpu.VMEM(shape, jnp.float32)

        one, three = f32(PLANES, ROWS, 128), f32(3, PLANES, ROWS, 128)
        q1, q3 = f32(6, COARSE_ROWS, 128), f32(3, 6, COARSE_ROWS, 128)
        scratch = [
            f32(3, 8, 32, 128),
            pltpu.VMEM((8, 32, 128), jnp.int32),
            f32(8, 32, 128),
            *[one] * 5,
            *[three] * 11,
            *[three] * 7,
            f32(3, 8, ROWS, 128),
            *[f32(2, 96, 128)] * 2,
            *[f32(2, 40, 128)] * 2,
            *[f32(2, 72, 128)] * 2,
            *[f32(2, 32, 128)] * 2,
            f32(2, 2, COARSE_ROWS, 128),
            *[f32(2, 3, 2, COARSE_ROWS, 128)] * 2,
            *[q1] * 3,
            *[q3] * 5,
            *[q3] * 7,
            pltpu.SemaphoreType.DMA((4,)),
            pltpu.SemaphoreType.DMA((MESSAGES, 5)),
            pltpu.SemaphoreType.DMA((MESSAGES, 5)),
        ]
        hbm = pl.BlockSpec(memory_space=pl.ANY)
        return pl.pallas_call(
            functools.partial(kernel, bricks),
            out_shape=jax.ShapeDtypeStruct(prescribed.shape, jnp.float32),
            in_specs=[hbm] * 3,
            out_specs=hbm,
            scratch_shapes=scratch,
            compiler_params=pltpu.CompilerParams(collective_id=0, has_side_effects=True, vmem_limit_bytes=58 * 2**20),
        )(stiffness, prescribed, pinned)

    return jax.shard_map(
        body,
        mesh=mesh,
        in_specs=(P("band", "brick", None), P(None, "band", "brick", None), P("band", "brick", None)),
        out_specs=P(None, "band", "brick", None),
        check_vma=False,
    )
```

```python
import functools

import jax
import jax.numpy as jnp
from jax import lax
from jax.experimental import pallas as pl
from jax.experimental.pallas import tpu as pltpu
from jax.sharding import PartitionSpec as P

MESH = pl.DeviceIdType.MESH
PLANES = 13
ROWS = 48
COARSE_ROWS = 32
CHUNK = 2
BAND, UP, DOWN, DIAG_UP, DIAG_DOWN = range(5)
MESSAGES = 10
M_IN, M_FACE_U, M_FACE_K, M_FACE_FREE, M_KC, M_LATE_K, M_LATE_FREE, M_T, M_U, M_T2 = range(MESSAGES)


def lane_iota():
    return lax.broadcasted_iota(jnp.int32, (1, 128), 1)


def roll(value, by):
    return pltpu.roll(value, by % 128, value.ndim - 1)


def z_pair(value, weights, step):
    low, high = weights
    return roll(value, step) * low, roll(value, -step) * high


def z_stage(field, scaled, work, p, m, r0, n, weights, step):
    zu, zv, dz = work[:3]
    planes, rows = pl.ds(p, m), pl.ds(r0, n)
    for c in range(3):
        u = field[c, planes, rows]
        left, right = z_pair(u, weights, step)
        zu[c, planes, rows] = u + (left + right)
        dz[c, planes, rows] = right - left
    for c in range(3):
        v = scaled[c, planes, rows]
        left, right = z_pair(v, weights, step)
        zv[c, planes, rows] = v + (left + right)


def y_stage(field, work, p, m, r0, n):
    zu, zv, dz, ep, em, ec, tv = work
    planes, mid, low, high = pl.ds(p, m), pl.ds(r0, n), pl.ds(r0 - 1, n), pl.ds(r0 + 1, n)
    for c in range(3):
        a = zu[c, planes, mid]
        a = (a + a) + (zu[c, planes, low] + zu[c, planes, high])
        twice = a + a
        if c == 0:
            g = 0.5 * (field[1, planes, high] - field[1, planes, low]) + dz[2, planes, mid]
        elif c == 1:
            g = 0.5 * (field[0, planes, high] - field[0, planes, low])
            twice = twice + (dz[2, planes, high] - dz[2, planes, low])
        else:
            g = dz[0, planes, mid]
            twice = twice + (dz[1, planes, high] - dz[1, planes, low])
        ep[c, planes, mid] = a + g
        em[c, planes, mid] = a - g
        ec[c, planes, mid] = twice
        v = zv[c, planes, mid]
        tv[c, planes, mid] = (v + v) + (zv[c, planes, low] + zv[c, planes, high])


def x_terms(field, k, g4, work, c, p, m, rows):
    ep, em, ec, tv = work[3:]
    here, before, after = pl.ds(p, m), pl.ds(p - 1, m), pl.ds(p + 1, m)
    e = (ep[c, after, rows] + em[c, before, rows]) + ec[c, here, rows]
    pairs = tv[c, pl.ds(p - 1, m + 1), rows] + tv[c, pl.ds(p, m + 1), rows]
    return (pairs[:-1] + pairs[1:]) + k * e - g4 * field[c, here, rows]


def kernel(
    bricks,
    stiff_in,
    pres_in,
    pin_in,
    out_hbm,
    pr_in,
    pin_own,
    k_own,
    k_f,
    free_f,
    fr8_f,
    g4_f,
    fh_f,
    ua,
    va,
    ub,
    vb,
    uc,
    ud,
    vd,
    ue,
    ve,
    res,
    out_f,
    *rest,
):
    work, work_2, rest = rest[:7], rest[7:14], rest[14:]
    (
        prolonged,
        in_pack,
        in_land,
        in_diag_pack,
        in_diag_land,
        u_pack,
        u_land,
        u_diag_pack,
        u_diag_land,
        kc,
        t_1,
        t_2,
        k_q,
        g_q,
        s_q,
        w_q,
        ca,
        cva,
        cb,
        cvb,
    ) = rest[:-10]
    coarse_work, (in_sem, send_sem, recv_sem) = rest[-10:-3], rest[-3:]
    b = lax.axis_index("band")
    i = lax.axis_index("brick")
    has_up, has_down = i > 0, i < bricks - 1
    own_plane = 1 + 3 * b
    planes_own = pl.ds(own_plane, 8)
    partners = {BAND: (1 - b, i), UP: (b, i - 1), DOWN: (b, i + 1), DIAG_UP: (1 - b, i - 1), DIAG_DOWN: (1 - b, i + 1)}

    locals_ = [
        pltpu.make_async_copy(stiff_in, k_own, in_sem.at[0]),
        pltpu.make_async_copy(pin_in, pin_own, in_sem.at[1]),
        pltpu.make_async_copy(pres_in, pr_in, in_sem.at[2]),
    ]
    for copy in locals_:
        copy.start()
    barrier = pltpu.get_barrier_semaphore()

    def greet(kind):
        pl.semaphore_signal(barrier, inc=1, device_id=partners[kind], device_id_type=MESH)

    greet(BAND)

    @pl.when(has_up)
    def _():
        greet(UP)
        greet(DIAG_UP)

    @pl.when(has_down)
    def _():
        greet(DOWN)
        greet(DIAG_DOWN)

    def outside(slot, rows):
        for ref in (in_land, in_diag_land, u_land, u_diag_land):
            ref[slot] = jnp.zeros(ref.shape[1:], jnp.float32)
        for band in range(2):
            for half in range(2):
                kc[band, half, rows] = jnp.zeros((8, 128), jnp.float32)
                for comp in range(3):
                    t_1[band, comp, half, rows] = jnp.zeros((8, 128), jnp.float32)
                    t_2[band, comp, half, rows] = jnp.zeros((8, 128), jnp.float32)

    @pl.when(jnp.logical_not(has_up))
    def _():
        outside(1, pl.ds(0, 8))

    @pl.when(jnp.logical_not(has_down))
    def _():
        outside(0, pl.ds(24, 8))

    outer = 12 * b
    k_f[outer] = jnp.zeros((ROWS, 128), jnp.float32)
    for ref in (*work[3:5], work[6], *work_2[3:5], work_2[6]):
        for comp in range(3):
            ref[comp, outer] = jnp.zeros((ROWS, 128), jnp.float32)

    lane = lane_iota()
    even = lax.rem(lane, 2) == 0
    fine_w = (jnp.where(lane == 0, 0.0, 0.5), jnp.where(lane == 127, 0.0, 0.5))
    coarse_w = (jnp.where(lane < 2, 0.0, 0.5), jnp.where(lane >= 126, 0.0, 0.5))

    def halve(load, first_row, emit):
        sums = []
        for x in range(4):
            p = 2 * x
            top, low = pl.ds(first_row, 16, stride=2), pl.ds(first_row + 1, 16, stride=2)
            sums.append((load(p, top) + load(p, low)) + (load(p + 1, top) + load(p + 1, low)))
        for half in range(2):
            first, second = sums[half], sums[half + 2]
            emit(half, jnp.where(even, first + roll(first, -1), second + roll(second, 1)))

    copies = {}

    def prepare(message, kind, src, dst):
        copies[message, kind] = pltpu.make_async_remote_copy(
            src_ref=src,
            dst_ref=dst,
            send_sem=send_sem.at[message, kind],
            recv_sem=recv_sem.at[message, kind],
            device_id=partners[kind],
            device_id_type=MESH,
        )

    def face_message(message, ref, depth, lead):
        src, dst = pl.ds(4 + (5 - depth) * (1 - b), depth), pl.ds((4 - depth) * (1 - b) + 9 * b, depth)
        rows = pl.ds(8, 32)
        if lead:
            prepare(message, BAND, ref.at[:, src, rows], ref.at[:, dst, rows])
        else:
            prepare(message, BAND, ref.at[src, rows], ref.at[dst, rows])

    def packed_messages(message, pack, land, diag_pack, diag_land):
        for slot, near, far in ((0, UP, DIAG_UP), (1, DOWN, DIAG_DOWN)):
            prepare(message, near, pack.at[slot], land.at[slot])
            prepare(message, far, diag_pack.at[slot], diag_land.at[slot])

    def coarse_messages(message, ref):
        def at(band, start, count):
            if len(ref.shape) == 4:
                return ref.at[band, :, pl.ds(start, count)]
            return ref.at[band, :, :, pl.ds(start, count)]

        prepare(message, BAND, at(0, 8, 16), at(1, 8, 16))
        prepare(message, UP, at(0, 8, 8), at(0, 24, 8))
        prepare(message, DIAG_UP, at(0, 8, 8), at(1, 24, 8))
        prepare(message, DOWN, at(0, 16, 8), at(0, 0, 8))
        prepare(message, DIAG_DOWN, at(0, 16, 8), at(1, 0, 8))

    packed_messages(M_IN, in_pack, in_land, in_diag_pack, in_diag_land)
    face_message(M_FACE_U, ua, 2, True)
    face_message(M_FACE_K, k_f, 2, False)
    face_message(M_FACE_FREE, free_f, 1, False)
    third, outer_two = pl.ds(1 + 10 * b, 1), pl.ds(1 + 9 * b, 2)
    prepare(M_LATE_K, BAND, k_f.at[pl.ds(6, 1), pl.ds(8, 32)], k_f.at[third, pl.ds(8, 32)])
    prepare(M_LATE_FREE, BAND, free_f.at[pl.ds(6 - b, 2), pl.ds(8, 32)], free_f.at[outer_two, pl.ds(8, 32)])
    coarse_messages(M_KC, kc)
    coarse_messages(M_T, t_1)
    coarse_messages(M_T2, t_2)
    packed_messages(M_U, u_pack, u_land, u_diag_pack, u_diag_land)
    face_message(M_U, uc, 3, True)

    def each(messages, act, above, below, far=True, near=True):
        for holds, kinds in ((above, (UP, DIAG_UP)), (below, (DOWN, DIAG_DOWN))):
            found = [copies[m, kind] for m in messages for kind in kinds if far and (m, kind) in copies]
            if found:

                @pl.when(holds)
                def _(found=found):
                    for copy in found:
                        act(copy)

        for m in messages:
            if near and (m, BAND) in copies:
                act(copies[m, BAND])

    def start(*messages):
        each(messages, lambda copy: copy.start(), has_up, has_down)

    def received(*messages, far=True, near=True):
        each(messages, lambda copy: copy.wait_recv(), has_down, has_up, far, near)

    def sent(*messages):
        each(messages, lambda copy: copy.wait_send(), has_up, has_down)

    def edges(slot, depth):
        return (pl.ds(8, depth), pl.ds(40, depth)) if slot == 0 else (pl.ds(40 - depth, depth), pl.ds(8 - depth, depth))

    def pack(fields, dst, diag_dst):
        total = sum(depth for _, depth in fields)
        face = own_plane + 5 * (1 - b)
        for slot in range(2):
            at = 0
            for load, depth in fields:
                rows = edges(slot, depth)[0]
                for q in range(8):
                    dst[slot, pl.ds(q * total + at, depth)] = load(own_plane + q, rows)
                for q in range(3):
                    diag_dst[slot, pl.ds(q * total + at, depth)] = load(face + q, rows)
                at += depth

    def unpack(fields, land, diag_land):
        total = sum(depth for _, depth in fields)
        face = 1 + 8 * (1 - b)
        for slot in range(2):
            at = 0
            for store, depth in fields:
                rows = edges(slot, depth)[1]
                for q in range(8):
                    store(own_plane + q, rows, land[slot, pl.ds(q * total + at, depth)])
                for q in range(3):
                    store(face + q, rows, diag_land[slot, pl.ds(q * total + at, depth)])
                at += depth

    def load_of(ref, comp=None):
        return (lambda p, rows: ref[p, rows]) if comp is None else (lambda p, rows: ref[comp, p, rows])

    def store_of(ref, comp=None):
        def store(p, rows, value):
            if comp is None:
                ref[p, rows] = value
            else:
                ref[comp, p, rows] = value

        return store

    for copy in locals_:
        copy.wait()
    own_rows = pl.ds(8, 32)
    for q in range(8):
        at = own_plane + q
        pinned = pin_own[q].astype(jnp.float32)
        free_f[at, own_rows] = 1.0 - pinned
        k = k_own[q]
        k_f[at, own_rows] = k
        for comp in range(3):
            u = pr_in[comp, q] * pinned
            ua[comp, at, own_rows] = u
            va[comp, at, own_rows] = k * u
    pack(
        [(load_of(ua, 0), 2), (load_of(ua, 1), 2), (load_of(ua, 2), 2), (load_of(k_f), 3), (load_of(free_f), 3)],
        in_pack,
        in_diag_pack,
    )

    def put_kc(half, value):
        kc[0, half, pl.ds(8, 16)] = 0.125 * value

    halve(lambda p, rows: k_own[p, rows], 0, put_kc)

    pl.semaphore_wait(barrier, 1 + 2 * has_up.astype(jnp.int32) + 2 * has_down.astype(jnp.int32))
    start(M_IN, M_KC, M_FACE_U, M_FACE_K, M_FACE_FREE, M_LATE_K, M_LATE_FREE)

    kz, ky = prolonged.at[0], prolonged.at[1]

    def k_z(p, m, r0, n):
        planes, rows = pl.ds(p, m), pl.ds(r0, n)
        k = k_f[planes, rows]
        left, right = z_pair(k, fine_w, 1)
        kz[planes, rows] = k + (left + right)

    def k_y(p, m, r0, n):
        planes = pl.ds(p, m)
        ky[planes, pl.ds(r0, n)] = kz[planes, pl.ds(r0, n)] + 0.5 * (
            kz[planes, pl.ds(r0 - 1, n)] + kz[planes, pl.ds(r0 + 1, n)]
        )

    def coefficients(p, m, r0, n):
        for q in range(0, m, CHUNK):
            size = min(CHUNK, m - q)
            at, rows = p + q, pl.ds(r0, n)
            here = pl.ds(at, size)
            k, free = k_f[here, rows], free_f[here, rows]
            t = ky[here, rows] + 0.5 * (ky[pl.ds(at - 1, size), rows] + ky[pl.ds(at + 1, size), rows])
            g4_f[here, rows] = 32.0 * k + 4.0 * t
            fr8_f[here, rows] = 0.03125 * free
            inside = k > 0.0
            fh_f[here, rows] = jnp.where(inside, 0.15 * free / jnp.where(inside, 6.0 * k + t, 1.0), 0.0)

    def x_stage(field, used, p, m, r0, n, emit):
        rows, here = pl.ds(r0, n), pl.ds(p, m)
        k, g4 = k_f[here, rows], g4_f[here, rows]
        for comp in range(3):
            emit(comp, here, rows, k, field, x_terms(field, k, g4, used, comp, p, m, rows))

    def fine(field, scaled, m, out_m, r0, n, emit, before=None):
        first = 1 - b
        done = 0

        def start_of(q, size):
            return (1 + q) * first + (12 - q - size) * b

        for q in range(0, m, CHUNK):
            if before is not None and before[0] == q:
                before[1]()
            size = min(CHUNK, m - q)
            z_stage(field, scaled, work, start_of(q, size), size, r0 - 1, n + 2, fine_w, 1)
            y_stage(field, work, start_of(q, size), size, r0, n)
            while done < out_m:
                out_size = min(CHUNK, out_m - done)
                if q + size < min(m, done + out_size + 1):
                    break
                x_stage(field, work, start_of(done, out_size), out_size, r0, n, emit)
                done += out_size

    def sweep_to(out_u, out_v):
        def emit(comp, here, rows, k, field, terms):
            u = field[comp, here, rows] + fh_f[here, rows] * terms
            out_u[comp, here, rows] = u
            if out_v is not None:
                out_v[comp, here, rows] = u * k

        return emit

    def to_residual(comp, here, rows, k, field, terms):
        res[comp, here, rows] = fr8_f[here, rows] * terms

    for ref in (kz, ky):
        ref[outer] = jnp.zeros((ROWS, 128), jnp.float32)
    all_but_1, all_but_2 = own_plane + b, own_plane + 2 * b
    halo_2, across_2, last_2 = 9 - 7 * b, 8 - 5 * b, 7 - 3 * b
    first_sweep = sweep_to(ub, vb)
    k_z(own_plane, 8, 8, 32)
    k_y(own_plane, 8, 9, 30)
    coefficients(all_but_1, 7, 9, 30)
    for q in range(0, 8, CHUNK):
        z_stage(ua, va, work, own_plane + q, CHUNK, 8, 32, fine_w, 1)
        y_stage(ua, work, own_plane + q, CHUNK, 9, 30)
    for q in range(7):
        x_stage(ua, work, all_but_1 + q, 1, 9, 30, first_sweep)
    for q in range(7):
        z_stage(ub, vb, work_2, all_but_1 + q, 1, 9, 30, fine_w, 1)
        y_stage(ub, work_2, all_but_1 + q, 1, 10, 28)
    for q in range(0, 6, CHUNK):
        x_stage(ub, work_2, all_but_2 + q, CHUNK, 10, 28, to_residual)

    received(M_IN, M_FACE_U, M_FACE_K, M_FACE_FREE)
    unpack(
        [(store_of(ua, 0), 2), (store_of(ua, 1), 2), (store_of(ua, 2), 2), (store_of(k_f), 3), (store_of(free_f), 3)],
        in_land,
        in_diag_land,
    )

    def scale(p, m, r0, n):
        planes, rows = pl.ds(p, m), pl.ds(r0, n)
        k = k_f[planes, rows]
        for comp in range(3):
            va[comp, planes, rows] = k * ua[comp, planes, rows]

    def strips(act, p, m, low, high, n):
        act(p, m, low, n)
        act(p, m, high, n)

    strips(scale, own_plane, 8, 6, 40, 2)
    scale(halo_2, 2, 6, 36)
    strips(k_z, own_plane, 8, 6, 40, 2)
    k_z(halo_2, 2, 6, 36)
    strips(k_y, own_plane, 8, 7, 39, 2)
    k_y(halo_2, 2, 7, 34)
    strips(coefficients, all_but_1, 7, 7, 39, 2)
    coefficients(across_2, 2, 7, 34)
    strips(lambda p, m, r0, n: z_stage(ua, va, work, p, m, r0, n, fine_w, 1), own_plane, 8, 6, 40, 2)
    z_stage(ua, va, work, halo_2, 2, 6, 36, fine_w, 1)
    strips(lambda p, m, r0, n: y_stage(ua, work, p, m, r0, n), own_plane, 8, 7, 39, 2)
    y_stage(ua, work, halo_2, 2, 7, 34)
    strips(lambda p, m, r0, n: x_stage(ua, work, p, m, r0, n, first_sweep), all_but_1, 7, 7, 39, 2)
    x_stage(ua, work, across_2, 2, 7, 34, first_sweep)
    strips(lambda p, m, r0, n: z_stage(ub, vb, work_2, p, m, r0, n, fine_w, 1), all_but_1, 7, 7, 39, 2)
    z_stage(ub, vb, work_2, across_2, 2, 7, 34, fine_w, 1)
    strips(lambda p, m, r0, n: y_stage(ub, work_2, p, m, r0, n), all_but_1, 7, 8, 38, 2)
    y_stage(ub, work_2, across_2, 2, 8, 32)
    strips(lambda p, m, r0, n: x_stage(ub, work_2, p, m, r0, n, to_residual), all_but_2, 6, 8, 38, 2)
    x_stage(ub, work_2, last_2, 2, 8, 32, to_residual)

    def put_target(dst):
        for comp in range(3):

            def put(half, value, comp=comp):
                dst[0, comp, half, pl.ds(8, 16)] = value

            halve(lambda p, rows, comp=comp: res[comp, own_plane + p, rows], 8, put)

    put_target(t_1)
    start(M_T)
    for comp in range(3):
        uc[comp, planes_own, own_rows] = ub[comp, planes_own, own_rows]
    u_fields = [(load_of(ub, 0), 3), (load_of(ub, 1), 3), (load_of(ub, 2), 3)]
    pack(u_fields, u_pack, u_diag_pack)
    start(M_U)

    def repack(load, rows, emit):
        for half in range(2):
            low, high = load(b, half, rows), load(1 - b, half, rows)
            emit(1 + half, jnp.where(even, low, roll(high, 1)))
            emit(3 + half, jnp.where(even, roll(low, -1), high))

    def wrap_after(value):
        return jnp.where(even, roll(value, -1), 0.0)

    def wrap_before(value):
        return jnp.where(even, 0.0, roll(value, 1))

    received(M_LATE_K, M_LATE_FREE)
    for q in range(0, 11, CHUNK):
        size = min(CHUNK, 11 - q)
        k_z(1 + q, size, 5, 38)
        k_y(1 + q, size, 6, 36)
    coefficients(1 + b, 10, 6, 36)

    received(M_KC)

    def put_kq(q, value):
        k_q[q, pl.ds(2, 28)] = value

    repack(lambda slot, half, rows: kc[slot, half, rows], pl.ds(2, 28), put_kq)
    czu, ctv = coarse_work[0], coarse_work[6]
    for q in range(1, 5):
        k = k_q[q, pl.ds(2, 28)]
        left, right = z_pair(k, coarse_w, 2)
        czu[0, q, pl.ds(2, 28)] = k + (left + right)
    whole = pl.ds(3, 26)
    for q in range(1, 5):
        ctv[0, q, whole] = czu[0, q, whole] + 0.5 * (czu[0, q, pl.ds(2, 26)] + czu[0, q, pl.ds(4, 26)])
    ctv[0, 5, whole] = wrap_after(ctv[0, 1, whole])
    ctv[0, 0, whole] = wrap_before(ctv[0, 4, whole])
    for q in range(1, 5):
        k = k_q[q, whole]
        t = ctv[0, q, whole] + 0.5 * (ctv[0, q - 1, whole] + ctv[0, q + 1, whole])
        g_q[q, whole] = 32.0 * k + 4.0 * t
        s_q[q, whole] = jnp.where(k > 0.0, 0.15 / jnp.where(k > 0.0, 6.0 * k + t, 1.0), 0.0)

    def coarse_sweep(field, scaled, out_u, out_v, r0, n):
        z_stage(field, scaled, coarse_work, 1, 4, r0 - 1, n + 2, coarse_w, 2)
        y_stage(field, coarse_work, 1, 4, r0, n)
        cep, cem, _, ctv = coarse_work[3:]
        rows = pl.ds(r0, n)
        for comp in range(3):
            cep[comp, 5, rows] = wrap_after(cep[comp, 1, rows])
            cem[comp, 0, rows] = wrap_before(cem[comp, 4, rows])
            ctv[comp, 5, rows] = wrap_after(ctv[comp, 1, rows])
            ctv[comp, 0, rows] = wrap_before(ctv[comp, 4, rows])
        here = pl.ds(1, 4)
        k, g4, s = k_q[here, rows], g_q[here, rows], s_q[here, rows]
        for comp in range(3):
            terms = x_terms(field, k, g4, coarse_work, comp, 1, 4, rows)
            u = field[comp, here, rows] + (w_q[comp, here, rows] + s * terms)
            out_u[comp, here, rows] = u
            if out_v is not None:
                out_v[comp, here, rows] = u * k

    def coarse(target, r0, n):
        rows = pl.ds(r0, n)
        for comp in range(3):

            def put(q, value, comp=comp):
                w = 16.0 * s_q[q, rows] * value
                w_q[comp, q, rows] = w
                ca[comp, q, rows] = w
                cva[comp, q, rows] = w * k_q[q, rows]

            repack(lambda slot, half, at, comp=comp: target[slot, comp, half, at], rows, put)
        coarse_sweep(ca, cva, cb, cvb, r0 + 1, n - 2)
        coarse_sweep(cb, cvb, ca, cva, r0 + 2, n - 4)
        coarse_sweep(ca, cva, cb, None, r0 + 3, n - 6)
        last, count = r0 + 3, n - 6
        for comp in range(3):
            for q in range(1, 5):
                value = cb[comp, q, pl.ds(last, count)]
                for x, part in ((q - 1, jnp.where(even, value, roll(value, 1))), (q + 3, jnp.where(even, roll(value, -1), value))):
                    prolonged[comp, x, pl.ds(2 * last - 8, count, stride=2)] = part
                    prolonged[comp, x, pl.ds(2 * last - 7, count, stride=2)] = part

    def correct(field, out_u, out_v, p, m, r0, n):
        rows = pl.ds(r0, n)
        for q in range(m):
            at = p + q
            x = (at - 1 + 5 * b) // 2
            k, free = k_f[at, rows], free_f[at, rows]
            for comp in range(3):
                u = field[comp, at, rows] + free * prolonged[comp, x, rows]
                out_u[comp, at, rows] = u
                out_v[comp, at, rows] = u * k

    received(M_T)
    coarse(t_1, 3, 26)
    received(M_U, near=False)
    unpack([(store_of(uc, 0), 3), (store_of(uc, 1), 3), (store_of(uc, 2), 3)], u_land, u_diag_land)
    correct(uc, ud, vd, own_plane, 8, 5, 38)

    def partner_planes():
        received(M_U, far=False)
        correct(uc, ud, vd, 9 - 8 * b, 3, 5, 38)

    fine(ud, vd, 11, 10, 6, 36, sweep_to(ue, ve), (8, partner_planes))

    fine(ue, ve, 10, 9, 7, 34, sweep_to(ud, vd))
    fine(ud, vd, 9, 8, 8, 32, to_residual)
    put_target(t_2)
    start(M_T2)
    received(M_T2)
    coarse(t_2, 4, 24)
    correct(ud, ue, ve, 1 + 2 * b, 9, 7, 34)
    fine(ue, ve, 9, 8, 8, 32, sweep_to(out_f, None))
    result = pltpu.make_async_copy(out_f.at[:, planes_own, own_rows], out_hbm, in_sem.at[3])
    result.start()
    sent(*range(MESSAGES))
    result.wait()


def solution(mesh):
    bricks = mesh.shape["brick"]

    def body(stiffness, prescribed, pinned):
        def f32(*shape):
            return pltpu.VMEM(shape, jnp.float32)

        one, three = f32(PLANES, ROWS, 128), f32(3, PLANES, ROWS, 128)
        q1, q3 = f32(6, COARSE_ROWS, 128), f32(3, 6, COARSE_ROWS, 128)
        scratch = [
            f32(3, 8, 32, 128),
            pltpu.VMEM((8, 32, 128), jnp.int32),
            f32(8, 32, 128),
            *[one] * 5,
            *[three] * 11,
            *[three] * 14,
            f32(3, PLANES, ROWS, 128),
            *[f32(2, 96, 128)] * 2,
            *[f32(2, 40, 128)] * 2,
            *[f32(2, 72, 128)] * 2,
            *[f32(2, 32, 128)] * 2,
            f32(2, 2, COARSE_ROWS, 128),
            *[f32(2, 3, 2, COARSE_ROWS, 128)] * 2,
            *[q1] * 3,
            *[q3] * 5,
            *[q3] * 7,
            pltpu.SemaphoreType.DMA((4,)),
            pltpu.SemaphoreType.DMA((MESSAGES, 5)),
            pltpu.SemaphoreType.DMA((MESSAGES, 5)),
        ]
        hbm = pl.BlockSpec(memory_space=pl.ANY)
        return pl.pallas_call(
            functools.partial(kernel, bricks),
            out_shape=jax.ShapeDtypeStruct(prescribed.shape, jnp.float32),
            in_specs=[hbm] * 3,
            out_specs=hbm,
            scratch_shapes=scratch,
            compiler_params=pltpu.CompilerParams(collective_id=0, has_side_effects=True, vmem_limit_bytes=58 * 2**20),
        )(stiffness, prescribed, pinned)

    return jax.shard_map(
        body,
        mesh=mesh,
        in_specs=(P("band", "brick", None), P(None, "band", "brick", None), P("band", "brick", None)),
        out_specs=P(None, "band", "brick", None),
        check_vma=False,
    )
```

```python
import functools

import jax
import jax.numpy as jnp
from jax import lax
from jax.experimental import pallas as pl
from jax.experimental.pallas import tpu as pltpu
from jax.sharding import PartitionSpec as P

MESH = pl.DeviceIdType.MESH
PLANES = 13
ROWS = 48
COARSE_ROWS = 32
CHUNK = 2
BAND, UP, DOWN, DIAG_UP, DIAG_DOWN = range(5)
MESSAGES = 12
M_IN, M_FACE_U, M_FACE_K, M_FACE_FREE, M_KC, M_LATE, M_LATE_K, M_LATE_FREE, M_U, M_T, M_FACE_U1, M_T2 = range(MESSAGES)


def lane_iota():
    return lax.broadcasted_iota(jnp.int32, (1, 128), 1)


def roll(value, by):
    return pltpu.roll(value, by % 128, value.ndim - 1)


def z_pair(value, weights, step):
    low, high = weights
    return roll(value, step) * low, roll(value, -step) * high


def z_stage(field, scaled, work, p, m, r0, n, weights, step):
    zu, zv, dz = work[:3]
    planes, rows = pl.ds(p, m), pl.ds(r0, n)
    for c in range(3):
        u = field[c, planes, rows]
        left, right = z_pair(u, weights, step)
        zu[c, planes, rows] = u + (left + right)
        dz[c, planes, rows] = right - left
    for c in range(3):
        v = scaled[c, planes, rows]
        left, right = z_pair(v, weights, step)
        zv[c, planes, rows] = v + (left + right)


def y_stage(field, work, p, m, r0, n):
    zu, zv, dz, ep, em, ec, tv = work
    planes, mid, low, high = pl.ds(p, m), pl.ds(r0, n), pl.ds(r0 - 1, n), pl.ds(r0 + 1, n)
    for c in range(3):
        a = zu[c, planes, mid]
        a = (a + a) + (zu[c, planes, low] + zu[c, planes, high])
        twice = a + a
        if c == 0:
            g = 0.5 * (field[1, planes, high] - field[1, planes, low]) + dz[2, planes, mid]
        elif c == 1:
            g = 0.5 * (field[0, planes, high] - field[0, planes, low])
            twice = twice + (dz[2, planes, high] - dz[2, planes, low])
        else:
            g = dz[0, planes, mid]
            twice = twice + (dz[1, planes, high] - dz[1, planes, low])
        ep[c, planes, mid] = a + g
        em[c, planes, mid] = a - g
        ec[c, planes, mid] = twice
        v = zv[c, planes, mid]
        tv[c, planes, mid] = (v + v) + (zv[c, planes, low] + zv[c, planes, high])


def x_terms(field, k, g4, work, c, p, m, rows):
    ep, em, ec, tv = work[3:]
    here, before, after = pl.ds(p, m), pl.ds(p - 1, m), pl.ds(p + 1, m)
    e = (ep[c, after, rows] + em[c, before, rows]) + ec[c, here, rows]
    pairs = tv[c, pl.ds(p - 1, m + 1), rows] + tv[c, pl.ds(p, m + 1), rows]
    return (pairs[:-1] + pairs[1:]) + k * e - g4 * field[c, here, rows]


def kernel(
    bricks,
    stiff_in,
    pres_in,
    pin_in,
    out_hbm,
    pr_in,
    pin_own,
    k_own,
    k_f,
    free_f,
    fr8_f,
    g4_f,
    fh_f,
    ua,
    va,
    ub,
    vb,
    uc,
    ud,
    vd,
    ue,
    ve,
    res,
    out_f,
    *rest,
):
    work, work_2, rest = rest[:7], rest[7:14], rest[14:]
    (
        prolonged,
        in_pack,
        in_land,
        in_diag_pack,
        in_diag_land,
        late_pack,
        late_land,
        late_diag_pack,
        late_diag_land,
        u_pack,
        u_land,
        u_diag_pack,
        u_diag_land,
        kc,
        t_1,
        t_2,
        t1_pack,
        t1_land,
        t2_pack,
        t2_land,
        k_q,
        g_q,
        s_q,
        w_q,
        ca,
        cva,
        cb,
        cvb,
    ) = rest[:-10]
    coarse_work, (in_sem, send_sem, recv_sem) = rest[-10:-3], rest[-3:]
    b = lax.axis_index("band")
    i = lax.axis_index("brick")
    has_up, has_down = i > 0, i < bricks - 1
    own_plane = 1 + 3 * b
    planes_own = pl.ds(own_plane, 8)
    partners = {BAND: (1 - b, i), UP: (b, i - 1), DOWN: (b, i + 1), DIAG_UP: (1 - b, i - 1), DIAG_DOWN: (1 - b, i + 1)}

    locals_ = [
        pltpu.make_async_copy(stiff_in, k_own, in_sem.at[0]),
        pltpu.make_async_copy(pin_in, pin_own, in_sem.at[1]),
        pltpu.make_async_copy(pres_in, pr_in, in_sem.at[2]),
    ]
    for copy in locals_:
        copy.start()
    barrier = pltpu.get_barrier_semaphore()

    def greet(kind):
        pl.semaphore_signal(barrier, inc=1, device_id=partners[kind], device_id_type=MESH)

    greet(BAND)

    @pl.when(has_up)
    def _():
        greet(UP)
        greet(DIAG_UP)

    @pl.when(has_down)
    def _():
        greet(DOWN)
        greet(DIAG_DOWN)

    def outside(slot, rows):
        for ref in (in_land, in_diag_land, late_land, late_diag_land, u_land, u_diag_land):
            ref[slot] = jnp.zeros(ref.shape[1:], jnp.float32)
        for ref in (t1_land, t2_land):
            for band in range(2):
                ref[slot, band] = jnp.zeros(ref.shape[2:], jnp.float32)
        for band in range(2):
            for half in range(2):
                kc[band, half, rows] = jnp.zeros((8, 128), jnp.float32)

    @pl.when(jnp.logical_not(has_up))
    def _():
        outside(1, pl.ds(0, 8))

    @pl.when(jnp.logical_not(has_down))
    def _():
        outside(0, pl.ds(24, 8))

    outer = 12 * b
    k_f[outer] = jnp.zeros((ROWS, 128), jnp.float32)
    for ref in (*work[3:5], work[6], *work_2[3:5], work_2[6]):
        for comp in range(3):
            ref[comp, outer] = jnp.zeros((ROWS, 128), jnp.float32)

    lane = lane_iota()
    even = lax.rem(lane, 2) == 0
    fine_w = (jnp.where(lane == 0, 0.0, 0.5), jnp.where(lane == 127, 0.0, 0.5))
    coarse_w = (jnp.where(lane < 2, 0.0, 0.5), jnp.where(lane >= 126, 0.0, 0.5))

    def halve(load, first_row, emit):
        sums = []
        for x in range(4):
            p = 2 * x
            top, low = pl.ds(first_row, 16, stride=2), pl.ds(first_row + 1, 16, stride=2)
            sums.append((load(p, top) + load(p, low)) + (load(p + 1, top) + load(p + 1, low)))
        for half in range(2):
            first, second = sums[half], sums[half + 2]
            emit(half, jnp.where(even, first + roll(first, -1), second + roll(second, 1)))

    copies = {}

    def prepare(message, kind, src, dst):
        copies[message, kind] = pltpu.make_async_remote_copy(
            src_ref=src,
            dst_ref=dst,
            send_sem=send_sem.at[message, kind],
            recv_sem=recv_sem.at[message, kind],
            device_id=partners[kind],
            device_id_type=MESH,
        )

    def face_message(message, ref, depth, lead):
        src, dst = pl.ds(4 + (5 - depth) * (1 - b), depth), pl.ds((4 - depth) * (1 - b) + 9 * b, depth)
        rows = pl.ds(8, 32)
        if lead:
            prepare(message, BAND, ref.at[:, src, rows], ref.at[:, dst, rows])
        else:
            prepare(message, BAND, ref.at[src, rows], ref.at[dst, rows])

    def packed_messages(message, pack, land, diag_pack, diag_land):
        for slot, near, far in ((0, UP, DIAG_UP), (1, DOWN, DIAG_DOWN)):
            prepare(message, near, pack.at[slot], land.at[slot])
            prepare(message, far, diag_pack.at[slot], diag_land.at[slot])

    def coarse_messages(message, ref):
        def at(band, start, count):
            return ref.at[band, :, pl.ds(start, count)]

        prepare(message, BAND, at(0, 8, 16), at(1, 8, 16))
        prepare(message, UP, at(0, 8, 8), at(0, 24, 8))
        prepare(message, DIAG_UP, at(0, 8, 8), at(1, 24, 8))
        prepare(message, DOWN, at(0, 16, 8), at(0, 0, 8))
        prepare(message, DIAG_DOWN, at(0, 16, 8), at(1, 0, 8))

    def target_messages(message, ref, packed, land):
        prepare(message, BAND, ref.at[0, :, :, pl.ds(8, 16)], ref.at[1, :, :, pl.ds(8, 16)])
        for slot, same, other in ((0, UP, DIAG_UP), (1, DOWN, DIAG_DOWN)):
            prepare(message, same, packed.at[slot], land.at[slot, 0])
            prepare(message, other, packed.at[slot], land.at[slot, 1])

    packed_messages(M_IN, in_pack, in_land, in_diag_pack, in_diag_land)
    face_message(M_FACE_U, ua, 2, True)
    face_message(M_FACE_K, k_f, 2, False)
    face_message(M_FACE_FREE, free_f, 1, False)
    third, outer_two = pl.ds(1 + 10 * b, 1), pl.ds(1 + 9 * b, 2)
    prepare(M_LATE_K, BAND, k_f.at[pl.ds(6, 1), pl.ds(8, 32)], k_f.at[third, pl.ds(8, 32)])
    prepare(M_LATE_FREE, BAND, free_f.at[pl.ds(6 - b, 2), pl.ds(8, 32)], free_f.at[outer_two, pl.ds(8, 32)])
    coarse_messages(M_KC, kc)
    target_messages(M_T, t_1, t1_pack, t1_land)
    target_messages(M_T2, t_2, t2_pack, t2_land)
    packed_messages(M_LATE, late_pack, late_land, late_diag_pack, late_diag_land)
    packed_messages(M_U, u_pack, u_land, u_diag_pack, u_diag_land)
    face_message(M_FACE_U1, uc, 3, True)

    def each(messages, act, above, below):
        for holds, kinds in ((above, (UP, DIAG_UP)), (below, (DOWN, DIAG_DOWN))):
            found = [copies[m, kind] for m in messages for kind in kinds if (m, kind) in copies]
            if found:

                @pl.when(holds)
                def _(found=found):
                    for copy in found:
                        act(copy)

        for m in messages:
            if (m, BAND) in copies:
                act(copies[m, BAND])

    def start(*messages):
        each(messages, lambda copy: copy.start(), has_up, has_down)

    def received(*messages):
        each(messages, lambda copy: copy.wait_recv(), has_down, has_up)

    def sent(*messages):
        each(messages, lambda copy: copy.wait_send(), has_up, has_down)

    def edge(slot, depth, skip):
        if slot == 0:
            return pl.ds(8 + skip, depth), pl.ds(40 + skip, depth)
        return pl.ds(40 - skip - depth, depth), pl.ds(8 - skip - depth, depth)

    def pieces(fields, count):
        total = sum(depth for _, depth, _ in fields)
        for slot in range(2):
            at = 0
            for access, depth, skip in fields:
                out_rows, in_rows = edge(slot, depth, skip)
                for q in range(count):
                    yield slot, q, access, out_rows, in_rows, pl.ds(q * total + at, depth)
                at += depth

    def pack(fields, dst):
        for slot, q, load, rows, _, at in pieces(fields, 8):
            dst[slot, at] = load(own_plane + q, rows)

    def pack_diag(fields, dst, count):
        face = own_plane + (8 - count) * (1 - b)
        for slot, q, load, rows, _, at in pieces(fields, count):
            dst[slot, at] = load(face + q, rows)

    def unpack(fields, land):
        for slot, q, store, _, rows, at in pieces(fields, 8):
            store(own_plane + q, rows, land[slot, at])

    def unpack_diag(fields, land, count):
        face = (4 - count) * b + 9 * (1 - b)
        for slot, q, store, _, rows, at in pieces(fields, count):
            store(face + q, rows, land[slot, at])

    def load_of(ref, comp=None):
        return (lambda p, rows: ref[p, rows]) if comp is None else (lambda p, rows: ref[comp, p, rows])

    def store_of(ref, comp=None):
        def store(p, rows, value):
            if comp is None:
                ref[p, rows] = value
            else:
                ref[comp, p, rows] = value

        return store

    for copy in locals_:
        copy.wait()
    own_rows = pl.ds(8, 32)
    for q in range(8):
        at = own_plane + q
        pinned = pin_own[q].astype(jnp.float32)
        free_f[at, own_rows] = 1.0 - pinned
        k = k_own[q]
        k_f[at, own_rows] = k
        for comp in range(3):
            u = pr_in[comp, q] * pinned
            ua[comp, at, own_rows] = u
            va[comp, at, own_rows] = k * u
    def early(of):
        return [(of(ua, 0), 2, 0), (of(ua, 1), 2, 0), (of(ua, 2), 2, 0), (of(k_f), 2, 0), (of(free_f), 1, 0)]

    def late(of):
        return [(of(k_f), 1, 2), (of(free_f), 2, 1)]

    def late_diag(of):
        return [(of(k_f), 3, 0), (of(free_f), 3, 0)]

    def rows_of_u1(of, ref):
        return [(of(ref, comp), 3, 0) for comp in range(3)]

    pack(early(load_of), in_pack)
    pack_diag(early(load_of), in_diag_pack, 2)
    pack(late(load_of), late_pack)
    pack_diag(late_diag(load_of), late_diag_pack, 3)

    def put_kc(half, value):
        kc[0, half, pl.ds(8, 16)] = 0.125 * value

    halve(lambda p, rows: k_own[p, rows], 0, put_kc)

    pl.semaphore_wait(barrier, 1 + 2 * has_up.astype(jnp.int32) + 2 * has_down.astype(jnp.int32))
    start(M_IN, M_FACE_U, M_FACE_K, M_FACE_FREE)
    start(M_KC, M_LATE, M_LATE_K, M_LATE_FREE)

    kz, ky = prolonged.at[0], prolonged.at[1]

    def k_z(p, m, r0, n):
        planes, rows = pl.ds(p, m), pl.ds(r0, n)
        k = k_f[planes, rows]
        left, right = z_pair(k, fine_w, 1)
        kz[planes, rows] = k + (left + right)

    def k_y(p, m, r0, n):
        planes = pl.ds(p, m)
        ky[planes, pl.ds(r0, n)] = kz[planes, pl.ds(r0, n)] + 0.5 * (
            kz[planes, pl.ds(r0 - 1, n)] + kz[planes, pl.ds(r0 + 1, n)]
        )

    def coefficients(p, m, r0, n):
        for q in range(0, m, CHUNK):
            size = min(CHUNK, m - q)
            at, rows = p + q, pl.ds(r0, n)
            here = pl.ds(at, size)
            k, free = k_f[here, rows], free_f[here, rows]
            t = ky[here, rows] + 0.5 * (ky[pl.ds(at - 1, size), rows] + ky[pl.ds(at + 1, size), rows])
            g4_f[here, rows] = 32.0 * k + 4.0 * t
            fr8_f[here, rows] = 0.03125 * free
            inside = k > 0.0
            fh_f[here, rows] = jnp.where(inside, 0.15 * free / jnp.where(inside, 6.0 * k + t, 1.0), 0.0)

    def x_stage(field, used, p, m, r0, n, emit):
        rows, here = pl.ds(r0, n), pl.ds(p, m)
        k, g4 = k_f[here, rows], g4_f[here, rows]
        for comp in range(3):
            emit(comp, here, rows, k, field, x_terms(field, k, g4, used, comp, p, m, rows))

    def fine(field, scaled, m, out_m, r0, n, emit, before=None):
        first = 1 - b
        done = 0

        def start_of(q, size):
            return (1 + q) * first + (12 - q - size) * b

        for q in range(0, m, CHUNK):
            if before is not None and before[0] == q:
                before[1]()
            size = min(CHUNK, m - q)
            z_stage(field, scaled, work, start_of(q, size), size, r0 - 1, n + 2, fine_w, 1)
            y_stage(field, work, start_of(q, size), size, r0, n)
            while done < out_m:
                out_size = min(CHUNK, out_m - done)
                if q + size < min(m, done + out_size + 1):
                    break
                x_stage(field, work, start_of(done, out_size), out_size, r0, n, emit)
                done += out_size

    def sweep_to(out_u, out_v):
        def emit(comp, here, rows, k, field, terms):
            u = field[comp, here, rows] + fh_f[here, rows] * terms
            out_u[comp, here, rows] = u
            if out_v is not None:
                out_v[comp, here, rows] = u * k

        return emit

    def to_residual(comp, here, rows, k, field, terms):
        res[comp, here, rows] = fr8_f[here, rows] * terms

    for ref in (kz, ky):
        ref[outer] = jnp.zeros((ROWS, 128), jnp.float32)
    all_but_1, all_but_2 = own_plane + b, own_plane + 2 * b
    halo_2, across_2, last_2 = 9 - 7 * b, 8 - 5 * b, 7 - 3 * b
    first_sweep = sweep_to(ub, vb)
    k_z(own_plane, 8, 8, 32)
    k_y(own_plane, 8, 9, 30)
    coefficients(all_but_1, 7, 9, 30)
    for q in range(0, 8, CHUNK):
        z_stage(ua, va, work, own_plane + q, CHUNK, 8, 32, fine_w, 1)
        y_stage(ua, work, own_plane + q, CHUNK, 9, 30)
    for q in range(7):
        x_stage(ua, work, all_but_1 + q, 1, 9, 30, first_sweep)
    for q in range(7):
        z_stage(ub, vb, work_2, all_but_1 + q, 1, 9, 30, fine_w, 1)
        y_stage(ub, work_2, all_but_1 + q, 1, 10, 28)
    for q in range(0, 6, CHUNK):
        x_stage(ub, work_2, all_but_2 + q, CHUNK, 10, 28, to_residual)

    received(M_IN, M_FACE_U, M_FACE_K, M_FACE_FREE)
    unpack(early(store_of), in_land)
    unpack_diag(early(store_of), in_diag_land, 2)

    def scale(p, m, r0, n):
        planes, rows = pl.ds(p, m), pl.ds(r0, n)
        k = k_f[planes, rows]
        for comp in range(3):
            va[comp, planes, rows] = k * ua[comp, planes, rows]

    def strips(act, p, m, low, high, n):
        act(p, m, low, n)
        act(p, m, high, n)

    strips(scale, own_plane, 8, 6, 40, 2)
    scale(halo_2, 2, 6, 36)
    strips(k_z, own_plane, 8, 6, 40, 2)
    k_z(halo_2, 2, 6, 36)
    strips(k_y, own_plane, 8, 7, 39, 2)
    k_y(halo_2, 2, 7, 34)
    strips(coefficients, all_but_1, 7, 7, 39, 2)
    coefficients(across_2, 2, 7, 34)
    strips(lambda p, m, r0, n: z_stage(ua, va, work, p, m, r0, n, fine_w, 1), own_plane, 8, 6, 40, 2)
    z_stage(ua, va, work, halo_2, 2, 6, 36, fine_w, 1)
    strips(lambda p, m, r0, n: y_stage(ua, work, p, m, r0, n), own_plane, 8, 7, 39, 2)
    y_stage(ua, work, halo_2, 2, 7, 34)
    strips(lambda p, m, r0, n: x_stage(ua, work, p, m, r0, n, first_sweep), all_but_1, 7, 7, 39, 2)
    x_stage(ua, work, across_2, 2, 7, 34, first_sweep)
    pack(rows_of_u1(load_of, ub), u_pack)
    pack_diag(rows_of_u1(load_of, ub), u_diag_pack, 3)
    start(M_U)
    strips(lambda p, m, r0, n: z_stage(ub, vb, work_2, p, m, r0, n, fine_w, 1), all_but_1, 7, 7, 39, 2)
    z_stage(ub, vb, work_2, across_2, 2, 7, 34, fine_w, 1)
    strips(lambda p, m, r0, n: y_stage(ub, work_2, p, m, r0, n), all_but_1, 7, 8, 38, 2)
    y_stage(ub, work_2, across_2, 2, 8, 32)
    strips(lambda p, m, r0, n: x_stage(ub, work_2, p, m, r0, n, to_residual), all_but_2, 6, 8, 38, 2)
    x_stage(ub, work_2, last_2, 2, 8, 32, to_residual)

    def put_target(dst, packed, depth):
        for comp in range(3):

            def put(half, value, comp=comp):
                dst[0, comp, half, pl.ds(8, 16)] = value

            halve(lambda p, rows, comp=comp: res[comp, own_plane + p, rows], 8, put)
            for half in range(2):
                at = pl.ds((2 * comp + half) * depth, depth)
                packed[0, at] = dst[0, comp, half, pl.ds(8, depth)]
                packed[1, at] = dst[0, comp, half, pl.ds(24 - depth, depth)]

    def far_target(dst, land, depth):
        for band in range(2):
            for comp in range(3):
                for half in range(2):
                    at = pl.ds((2 * comp + half) * depth, depth)
                    dst[band, comp, half, pl.ds(24, depth)] = land[0, band, at]
                    dst[band, comp, half, pl.ds(8 - depth, depth)] = land[1, band, at]

    put_target(t_1, t1_pack, 5)
    start(M_T)
    for comp in range(3):
        uc[comp, planes_own, own_rows] = ub[comp, planes_own, own_rows]
    start(M_FACE_U1)

    def repack(load, rows, emit):
        for half in range(2):
            low, high = load(b, half, rows), load(1 - b, half, rows)
            emit(1 + half, jnp.where(even, low, roll(high, 1)))
            emit(3 + half, jnp.where(even, roll(low, -1), high))

    def wrap_after(value):
        return jnp.where(even, roll(value, -1), 0.0)

    def wrap_before(value):
        return jnp.where(even, 0.0, roll(value, 1))

    received(M_LATE, M_LATE_K, M_LATE_FREE)
    unpack(late(store_of), late_land)
    unpack_diag(late_diag(store_of), late_diag_land, 3)
    for q in range(0, 11, CHUNK):
        size = min(CHUNK, 11 - q)
        k_z(1 + q, size, 5, 38)
        k_y(1 + q, size, 6, 36)
    coefficients(1 + b, 10, 6, 36)

    received(M_KC)

    def put_kq(q, value):
        k_q[q, pl.ds(2, 28)] = value

    repack(lambda slot, half, rows: kc[slot, half, rows], pl.ds(2, 28), put_kq)
    czu, ctv = coarse_work[0], coarse_work[6]
    for q in range(1, 5):
        k = k_q[q, pl.ds(2, 28)]
        left, right = z_pair(k, coarse_w, 2)
        czu[0, q, pl.ds(2, 28)] = k + (left + right)
    whole = pl.ds(3, 26)
    for q in range(1, 5):
        ctv[0, q, whole] = czu[0, q, whole] + 0.5 * (czu[0, q, pl.ds(2, 26)] + czu[0, q, pl.ds(4, 26)])
    ctv[0, 5, whole] = wrap_after(ctv[0, 1, whole])
    ctv[0, 0, whole] = wrap_before(ctv[0, 4, whole])
    for q in range(1, 5):
        k = k_q[q, whole]
        t = ctv[0, q, whole] + 0.5 * (ctv[0, q - 1, whole] + ctv[0, q + 1, whole])
        g_q[q, whole] = 32.0 * k + 4.0 * t
        s_q[q, whole] = jnp.where(k > 0.0, 0.15 / jnp.where(k > 0.0, 6.0 * k + t, 1.0), 0.0)

    def coarse_sweep(field, scaled, out_u, out_v, r0, n):
        z_stage(field, scaled, coarse_work, 1, 4, r0 - 1, n + 2, coarse_w, 2)
        y_stage(field, coarse_work, 1, 4, r0, n)
        cep, cem, _, ctv = coarse_work[3:]
        rows = pl.ds(r0, n)
        for comp in range(3):
            cep[comp, 5, rows] = wrap_after(cep[comp, 1, rows])
            cem[comp, 0, rows] = wrap_before(cem[comp, 4, rows])
            ctv[comp, 5, rows] = wrap_after(ctv[comp, 1, rows])
            ctv[comp, 0, rows] = wrap_before(ctv[comp, 4, rows])
        here = pl.ds(1, 4)
        k, g4, s = k_q[here, rows], g_q[here, rows], s_q[here, rows]
        for comp in range(3):
            terms = x_terms(field, k, g4, coarse_work, comp, 1, 4, rows)
            u = field[comp, here, rows] + (w_q[comp, here, rows] + s * terms)
            out_u[comp, here, rows] = u
            if out_v is not None:
                out_v[comp, here, rows] = u * k

    def coarse(target, r0, n):
        rows = pl.ds(r0, n)
        for comp in range(3):

            def put(q, value, comp=comp):
                w = 16.0 * s_q[q, rows] * value
                w_q[comp, q, rows] = w
                ca[comp, q, rows] = w
                cva[comp, q, rows] = w * k_q[q, rows]

            repack(lambda slot, half, at, comp=comp: target[slot, comp, half, at], rows, put)
        coarse_sweep(ca, cva, cb, cvb, r0 + 1, n - 2)
        coarse_sweep(cb, cvb, ca, cva, r0 + 2, n - 4)
        coarse_sweep(ca, cva, cb, None, r0 + 3, n - 6)
        last, count = r0 + 3, n - 6
        for comp in range(3):
            for q in range(1, 5):
                value = cb[comp, q, pl.ds(last, count)]
                for x, part in ((q - 1, jnp.where(even, value, roll(value, 1))), (q + 3, jnp.where(even, roll(value, -1), value))):
                    prolonged[comp, x, pl.ds(2 * last - 8, count, stride=2)] = part
                    prolonged[comp, x, pl.ds(2 * last - 7, count, stride=2)] = part

    def correct(field, out_u, out_v, p, m, r0, n):
        rows = pl.ds(r0, n)
        for q in range(m):
            at = p + q
            x = (at - 1 + 5 * b) // 2
            k, free = k_f[at, rows], free_f[at, rows]
            for comp in range(3):
                u = field[comp, at, rows] + free * prolonged[comp, x, rows]
                out_u[comp, at, rows] = u
                out_v[comp, at, rows] = u * k

    received(M_T)
    far_target(t_1, t1_land, 5)
    coarse(t_1, 3, 26)
    received(M_U)
    unpack(rows_of_u1(store_of, uc), u_land)
    unpack_diag(rows_of_u1(store_of, uc), u_diag_land, 3)
    correct(uc, ud, vd, own_plane, 8, 5, 38)

    def partner_planes():
        received(M_FACE_U1)
        correct(uc, ud, vd, 9 - 8 * b, 3, 5, 38)

    fine(ud, vd, 11, 10, 6, 36, sweep_to(ue, ve), (8, partner_planes))

    fine(ue, ve, 10, 9, 7, 34, sweep_to(ud, vd))
    fine(ud, vd, 9, 8, 8, 32, to_residual)
    put_target(t_2, t2_pack, 4)
    start(M_T2)
    received(M_T2)
    far_target(t_2, t2_land, 4)
    coarse(t_2, 4, 24)
    correct(ud, ue, ve, 1 + 2 * b, 9, 7, 34)
    fine(ue, ve, 9, 8, 8, 32, sweep_to(out_f, None))
    result = pltpu.make_async_copy(out_f.at[:, planes_own, own_rows], out_hbm, in_sem.at[3])
    result.start()
    sent(*range(MESSAGES))
    result.wait()


def solution(mesh):
    bricks = mesh.shape["brick"]

    def body(stiffness, prescribed, pinned):
        def f32(*shape):
            return pltpu.VMEM(shape, jnp.float32)

        one, three = f32(PLANES, ROWS, 128), f32(3, PLANES, ROWS, 128)
        q1, q3 = f32(6, COARSE_ROWS, 128), f32(3, 6, COARSE_ROWS, 128)
        scratch = [
            f32(3, 8, 32, 128),
            pltpu.VMEM((8, 32, 128), jnp.int32),
            f32(8, 32, 128),
            *[one] * 5,
            *[three] * 11,
            *[three] * 14,
            f32(3, PLANES, ROWS, 128),
            *[f32(2, 72, 128)] * 2,
            *[f32(2, 24, 128)] * 2,
            *[f32(2, 24, 128)] * 2,
            *[f32(2, 24, 128)] * 2,
            *[f32(2, 72, 128)] * 2,
            *[f32(2, 32, 128)] * 2,
            f32(2, 2, COARSE_ROWS, 128),
            *[f32(2, 3, 2, COARSE_ROWS, 128)] * 2,
            f32(2, 32, 128),
            f32(2, 2, 32, 128),
            f32(2, 24, 128),
            f32(2, 2, 24, 128),
            *[q1] * 3,
            *[q3] * 5,
            *[q3] * 7,
            pltpu.SemaphoreType.DMA((4,)),
            pltpu.SemaphoreType.DMA((MESSAGES, 5)),
            pltpu.SemaphoreType.DMA((MESSAGES, 5)),
        ]
        hbm = pl.BlockSpec(memory_space=pl.ANY)
        return pl.pallas_call(
            functools.partial(kernel, bricks),
            out_shape=jax.ShapeDtypeStruct(prescribed.shape, jnp.float32),
            in_specs=[hbm] * 3,
            out_specs=hbm,
            scratch_shapes=scratch,
            compiler_params=pltpu.CompilerParams(collective_id=0, has_side_effects=True, vmem_limit_bytes=58 * 2**20),
        )(stiffness, prescribed, pinned)

    return jax.shard_map(
        body,
        mesh=mesh,
        in_specs=(P("band", "brick", None), P(None, "band", "brick", None), P("band", "brick", None)),
        out_specs=P(None, "band", "brick", None),
        check_vma=False,
    )
```

```python
import functools

import jax
import jax.numpy as jnp
from jax import lax
from jax.experimental import pallas as pl
from jax.experimental.pallas import tpu as pltpu
from jax.sharding import PartitionSpec as P

MESH = pl.DeviceIdType.MESH
PLANES = 13
ROWS = 48
COARSE_ROWS = 32
CHUNK = 2
BAND, UP, DOWN, DIAG_UP, DIAG_DOWN = range(5)
MESSAGES = 12
M_IN, M_FACE_U, M_FACE_K, M_FACE_FREE, M_KC, M_LATE, M_LATE_K, M_LATE_FREE, M_U, M_T, M_FACE_U1, M_T2 = range(MESSAGES)


def lane_iota():
    return lax.broadcasted_iota(jnp.int32, (1, 128), 1)


def roll(value, by):
    return pltpu.roll(value, by % 128, value.ndim - 1)


def z_pair(value, weights, step):
    low, high = weights
    return roll(value, step) * low, roll(value, -step) * high


def z_stage(field, scaled, work, p, m, r0, n, weights, step):
    zu, zv, dz = work[:3]
    planes, rows = pl.ds(p, m), pl.ds(r0, n)
    for c in range(3):
        u = field[c, planes, rows]
        left, right = z_pair(u, weights, step)
        zu[c, planes, rows] = u + (left + right)
        dz[c, planes, rows] = right - left
    for c in range(3):
        v = scaled[c, planes, rows]
        left, right = z_pair(v, weights, step)
        zv[c, planes, rows] = v + (left + right)


def y_stage(field, work, p, m, r0, n):
    zu, zv, dz, ep, em, ec, tv = work
    planes, mid, low, high = pl.ds(p, m), pl.ds(r0, n), pl.ds(r0 - 1, n), pl.ds(r0 + 1, n)
    for c in range(3):
        a = zu[c, planes, mid]
        a = (a + a) + (zu[c, planes, low] + zu[c, planes, high])
        twice = a + a
        if c == 0:
            g = 0.5 * (field[1, planes, high] - field[1, planes, low]) + dz[2, planes, mid]
        elif c == 1:
            g = 0.5 * (field[0, planes, high] - field[0, planes, low])
            twice = twice + (dz[2, planes, high] - dz[2, planes, low])
        else:
            g = dz[0, planes, mid]
            twice = twice + (dz[1, planes, high] - dz[1, planes, low])
        ep[c, planes, mid] = a + g
        em[c, planes, mid] = a - g
        ec[c, planes, mid] = twice
        v = zv[c, planes, mid]
        tv[c, planes, mid] = (v + v) + (zv[c, planes, low] + zv[c, planes, high])


def x_terms(field, k, g4, work, c, p, m, rows):
    ep, em, ec, tv = work[3:]
    here, before, after = pl.ds(p, m), pl.ds(p - 1, m), pl.ds(p + 1, m)
    e = (ep[c, after, rows] + em[c, before, rows]) + ec[c, here, rows]
    pairs = tv[c, pl.ds(p - 1, m + 1), rows] + tv[c, pl.ds(p, m + 1), rows]
    return (pairs[:-1] + pairs[1:]) + k * e - g4 * field[c, here, rows]


def kernel(
    bricks,
    stiff_in,
    pres_in,
    pin_in,
    out_hbm,
    pr_in,
    pin_own,
    k_own,
    k_f,
    free_f,
    fr8_f,
    g4_f,
    fh_f,
    ua,
    va,
    ub,
    vb,
    uc,
    ud,
    vd,
    ue,
    ve,
    res,
    out_f,
    *rest,
):
    work, work_2, rest = rest[:7], rest[7:14], rest[14:]
    (
        prolonged,
        in_pack,
        in_land,
        in_diag_pack,
        in_diag_land,
        late_pack,
        late_land,
        late_diag_pack,
        late_diag_land,
        u_pack,
        u_land,
        u_diag_pack,
        u_diag_land,
        kc,
        t_1,
        t_2,
        t1_pack,
        t1_land,
        t2_pack,
        t2_land,
        k_q,
        g_q,
        s_q,
        w_q,
        ca,
        cva,
        cb,
        cvb,
    ) = rest[:-10]
    coarse_work, (in_sem, send_sem, recv_sem) = rest[-10:-3], rest[-3:]
    b = lax.axis_index("band")
    i = lax.axis_index("brick")
    has_up, has_down = i > 0, i < bricks - 1
    own_plane = 1 + 3 * b
    planes_own = pl.ds(own_plane, 8)
    partners = {BAND: (1 - b, i), UP: (b, i - 1), DOWN: (b, i + 1), DIAG_UP: (1 - b, i - 1), DIAG_DOWN: (1 - b, i + 1)}

    locals_ = [
        pltpu.make_async_copy(stiff_in, k_own, in_sem.at[0]),
        pltpu.make_async_copy(pin_in, pin_own, in_sem.at[1]),
        pltpu.make_async_copy(pres_in, pr_in, in_sem.at[2]),
    ]
    for copy in locals_:
        copy.start()
    barrier = pltpu.get_barrier_semaphore()

    def greet(kind):
        pl.semaphore_signal(barrier, inc=1, device_id=partners[kind], device_id_type=MESH)

    greet(BAND)

    @pl.when(has_up)
    def _():
        greet(UP)
        greet(DIAG_UP)

    @pl.when(has_down)
    def _():
        greet(DOWN)
        greet(DIAG_DOWN)

    def outside(slot, rows):
        for ref in (in_land, in_diag_land, late_land, late_diag_land, u_land, u_diag_land):
            ref[slot] = jnp.zeros(ref.shape[1:], jnp.float32)
        for ref in (t1_land, t2_land):
            for band in range(2):
                ref[slot, band] = jnp.zeros(ref.shape[2:], jnp.float32)
        for band in range(2):
            for half in range(2):
                kc[band, half, rows] = jnp.zeros((8, 128), jnp.float32)

    @pl.when(jnp.logical_not(has_up))
    def _():
        outside(1, pl.ds(0, 8))

    @pl.when(jnp.logical_not(has_down))
    def _():
        outside(0, pl.ds(24, 8))

    outer = 12 * b
    k_f[outer] = jnp.zeros((ROWS, 128), jnp.float32)
    for ref in (*work[3:5], work[6], *work_2[3:5], work_2[6]):
        for comp in range(3):
            ref[comp, outer] = jnp.zeros((ROWS, 128), jnp.float32)

    lane = lane_iota()
    even = lax.rem(lane, 2) == 0
    fine_w = (jnp.where(lane == 0, 0.0, 0.5), jnp.where(lane == 127, 0.0, 0.5))
    coarse_w = (jnp.where(lane < 2, 0.0, 0.5), jnp.where(lane >= 126, 0.0, 0.5))

    def halve(load, first_row, emit):
        sums = []
        for x in range(4):
            p = 2 * x
            top, low = pl.ds(first_row, 16, stride=2), pl.ds(first_row + 1, 16, stride=2)
            sums.append((load(p, top) + load(p, low)) + (load(p + 1, top) + load(p + 1, low)))
        for half in range(2):
            first, second = sums[half], sums[half + 2]
            emit(half, jnp.where(even, first + roll(first, -1), second + roll(second, 1)))

    copies = {}

    def prepare(message, kind, src, dst):
        copies[message, kind] = pltpu.make_async_remote_copy(
            src_ref=src,
            dst_ref=dst,
            send_sem=send_sem.at[message, kind],
            recv_sem=recv_sem.at[message, kind],
            device_id=partners[kind],
            device_id_type=MESH,
        )

    def face_message(message, ref, depth, lead):
        src, dst = pl.ds(4 + (5 - depth) * (1 - b), depth), pl.ds((4 - depth) * (1 - b) + 9 * b, depth)
        rows = pl.ds(8, 32)
        if lead:
            prepare(message, BAND, ref.at[:, src, rows], ref.at[:, dst, rows])
        else:
            prepare(message, BAND, ref.at[src, rows], ref.at[dst, rows])

    def packed_messages(message, pack, land, diag_pack, diag_land):
        for slot, near, far in ((0, UP, DIAG_UP), (1, DOWN, DIAG_DOWN)):
            prepare(message, near, pack.at[slot], land.at[slot])
            prepare(message, far, diag_pack.at[slot], diag_land.at[slot])

    def coarse_messages(message, ref):
        def at(band, start, count):
            return ref.at[band, :, pl.ds(start, count)]

        prepare(message, BAND, at(0, 8, 16), at(1, 8, 16))
        prepare(message, UP, at(0, 8, 8), at(0, 24, 8))
        prepare(message, DIAG_UP, at(0, 8, 8), at(1, 24, 8))
        prepare(message, DOWN, at(0, 16, 8), at(0, 0, 8))
        prepare(message, DIAG_DOWN, at(0, 16, 8), at(1, 0, 8))

    def target_messages(message, ref, packed, land):
        prepare(message, BAND, ref.at[0, :, :, pl.ds(8, 16)], ref.at[1, :, :, pl.ds(8, 16)])
        for slot, same, other in ((0, UP, DIAG_UP), (1, DOWN, DIAG_DOWN)):
            prepare(message, same, packed.at[slot], land.at[slot, 0])
            prepare(message, other, packed.at[slot], land.at[slot, 1])

    packed_messages(M_IN, in_pack, in_land, in_diag_pack, in_diag_land)
    face_message(M_FACE_U, ua, 2, True)
    face_message(M_FACE_K, k_f, 2, False)
    face_message(M_FACE_FREE, free_f, 1, False)
    third, outer_two = pl.ds(1 + 10 * b, 1), pl.ds(1 + 9 * b, 2)
    prepare(M_LATE_K, BAND, k_f.at[pl.ds(6, 1), pl.ds(8, 32)], k_f.at[third, pl.ds(8, 32)])
    prepare(M_LATE_FREE, BAND, free_f.at[pl.ds(6 - b, 2), pl.ds(8, 32)], free_f.at[outer_two, pl.ds(8, 32)])
    coarse_messages(M_KC, kc)
    target_messages(M_T, t_1, t1_pack, t1_land)
    target_messages(M_T2, t_2, t2_pack, t2_land)
    packed_messages(M_LATE, late_pack, late_land, late_diag_pack, late_diag_land)
    packed_messages(M_U, u_pack, u_land, u_diag_pack, u_diag_land)
    face_message(M_FACE_U1, uc, 3, True)

    def each(messages, act, above, below):
        for holds, kinds in ((above, (UP, DIAG_UP)), (below, (DOWN, DIAG_DOWN))):
            found = [copies[m, kind] for m in messages for kind in kinds if (m, kind) in copies]
            if found:

                @pl.when(holds)
                def _(found=found):
                    for copy in found:
                        act(copy)

        for m in messages:
            if (m, BAND) in copies:
                act(copies[m, BAND])

    def start(*messages):
        each(messages, lambda copy: copy.start(), has_up, has_down)

    def received(*messages):
        each(messages, lambda copy: copy.wait_recv(), has_down, has_up)

    def sent(*messages):
        each(messages, lambda copy: copy.wait_send(), has_up, has_down)

    def edge(slot, depth, skip):
        if slot == 0:
            return pl.ds(8 + skip, depth), pl.ds(40 + skip, depth)
        return pl.ds(40 - skip - depth, depth), pl.ds(8 - skip - depth, depth)

    def pieces(fields, count):
        total = sum(depth for _, depth, _ in fields)
        for slot in range(2):
            at = 0
            for access, depth, skip in fields:
                out_rows, in_rows = edge(slot, depth, skip)
                for q in range(count):
                    yield slot, q, access, out_rows, in_rows, pl.ds(q * total + at, depth)
                at += depth

    def pack(fields, dst):
        for slot, q, load, rows, _, at in pieces(fields, 8):
            dst[slot, at] = load(own_plane + q, rows)

    def pack_diag(fields, dst, count):
        face = own_plane + (8 - count) * (1 - b)
        for slot, q, load, rows, _, at in pieces(fields, count):
            dst[slot, at] = load(face + q, rows)

    def unpack(fields, land):
        for slot, q, store, _, rows, at in pieces(fields, 8):
            store(own_plane + q, rows, land[slot, at])

    def unpack_diag(fields, land, count):
        face = (4 - count) * b + 9 * (1 - b)
        for slot, q, store, _, rows, at in pieces(fields, count):
            store(face + q, rows, land[slot, at])

    def load_of(ref, comp=None):
        return (lambda p, rows: ref[p, rows]) if comp is None else (lambda p, rows: ref[comp, p, rows])

    def store_of(ref, comp=None):
        def store(p, rows, value):
            if comp is None:
                ref[p, rows] = value
            else:
                ref[comp, p, rows] = value

        return store

    for copy in locals_:
        copy.wait()
    own_rows = pl.ds(8, 32)
    for q in range(8):
        at = own_plane + q
        pinned = pin_own[q].astype(jnp.float32)
        free_f[at, own_rows] = 1.0 - pinned
        k = k_own[q]
        k_f[at, own_rows] = k
        for comp in range(3):
            u = pr_in[comp, q] * pinned
            ua[comp, at, own_rows] = u
    def early(of):
        return [(of(ua, 0), 2, 0), (of(ua, 1), 2, 0), (of(ua, 2), 2, 0), (of(k_f), 2, 0), (of(free_f), 1, 0)]

    def late(of):
        return [(of(k_f), 1, 2), (of(free_f), 2, 1)]

    def late_diag(of):
        return [(of(k_f), 3, 0), (of(free_f), 3, 0)]

    def rows_of_u1(of, ref):
        return [(of(ref, comp), 3, 0) for comp in range(3)]

    pack(early(load_of), in_pack)
    pack_diag(early(load_of), in_diag_pack, 2)

    pl.semaphore_wait(barrier, 1 + 2 * has_up.astype(jnp.int32) + 2 * has_down.astype(jnp.int32))
    start(M_IN, M_FACE_U, M_FACE_K, M_FACE_FREE)
    pack(late(load_of), late_pack)
    pack_diag(late_diag(load_of), late_diag_pack, 3)
    def put_kc(half, value):
        kc[0, half, pl.ds(8, 16)] = 0.125 * value

    halve(lambda p, rows: k_own[p, rows], 0, put_kc)
    start(M_KC, M_LATE, M_LATE_K, M_LATE_FREE)
    for q in range(8):
        at = own_plane + q
        for comp in range(3):
            va[comp, at, own_rows] = k_own[q] * ua[comp, at, own_rows]

    kz, ky = prolonged.at[0], prolonged.at[1]

    def k_z(p, m, r0, n):
        planes, rows = pl.ds(p, m), pl.ds(r0, n)
        k = k_f[planes, rows]
        left, right = z_pair(k, fine_w, 1)
        kz[planes, rows] = k + (left + right)

    def k_y(p, m, r0, n):
        planes = pl.ds(p, m)
        ky[planes, pl.ds(r0, n)] = kz[planes, pl.ds(r0, n)] + 0.5 * (
            kz[planes, pl.ds(r0 - 1, n)] + kz[planes, pl.ds(r0 + 1, n)]
        )

    def coefficients(p, m, r0, n):
        for q in range(0, m, CHUNK):
            size = min(CHUNK, m - q)
            at, rows = p + q, pl.ds(r0, n)
            here = pl.ds(at, size)
            k, free = k_f[here, rows], free_f[here, rows]
            t = ky[here, rows] + 0.5 * (ky[pl.ds(at - 1, size), rows] + ky[pl.ds(at + 1, size), rows])
            g4_f[here, rows] = 32.0 * k + 4.0 * t
            fr8_f[here, rows] = 0.03125 * free
            inside = k > 0.0
            fh_f[here, rows] = jnp.where(inside, 0.15 * free / jnp.where(inside, 6.0 * k + t, 1.0), 0.0)

    def x_stage(field, used, p, m, r0, n, emit):
        rows, here = pl.ds(r0, n), pl.ds(p, m)
        k, g4 = k_f[here, rows], g4_f[here, rows]
        for comp in range(3):
            emit(comp, here, rows, k, field, x_terms(field, k, g4, used, comp, p, m, rows))

    def fine(field, scaled, m, out_m, r0, n, emit, before=None):
        first = 1 - b
        done = 0

        def start_of(q, size):
            return (1 + q) * first + (12 - q - size) * b

        for q in range(0, m, CHUNK):
            if before is not None and before[0] == q:
                before[1]()
            size = min(CHUNK, m - q)
            z_stage(field, scaled, work, start_of(q, size), size, r0 - 1, n + 2, fine_w, 1)
            y_stage(field, work, start_of(q, size), size, r0, n)
            while done < out_m:
                out_size = min(CHUNK, out_m - done)
                if q + size < min(m, done + out_size + 1):
                    break
                x_stage(field, work, start_of(done, out_size), out_size, r0, n, emit)
                done += out_size

    def sweep_to(out_u, out_v):
        def emit(comp, here, rows, k, field, terms):
            u = field[comp, here, rows] + fh_f[here, rows] * terms
            out_u[comp, here, rows] = u
            if out_v is not None:
                out_v[comp, here, rows] = u * k

        return emit

    def to_residual(comp, here, rows, k, field, terms):
        res[comp, here, rows] = fr8_f[here, rows] * terms

    for ref in (kz, ky):
        ref[outer] = jnp.zeros((ROWS, 128), jnp.float32)
    all_but_1, all_but_2 = own_plane + b, own_plane + 2 * b
    halo_2, across_2, last_2 = 9 - 7 * b, 8 - 5 * b, 7 - 3 * b
    first_sweep = sweep_to(ub, vb)
    k_z(own_plane, 8, 8, 32)
    k_y(own_plane, 8, 9, 30)
    coefficients(all_but_1, 7, 9, 30)
    for q in range(0, 8, CHUNK):
        z_stage(ua, va, work, own_plane + q, CHUNK, 8, 32, fine_w, 1)
        y_stage(ua, work, own_plane + q, CHUNK, 9, 30)
    for q in range(7):
        x_stage(ua, work, all_but_1 + q, 1, 9, 30, first_sweep)
    for q in range(7):
        z_stage(ub, vb, work_2, all_but_1 + q, 1, 9, 30, fine_w, 1)
        y_stage(ub, work_2, all_but_1 + q, 1, 10, 28)
    for q in range(0, 6, CHUNK):
        x_stage(ub, work_2, all_but_2 + q, CHUNK, 10, 28, to_residual)

    received(M_IN, M_FACE_U, M_FACE_K, M_FACE_FREE)
    unpack(early(store_of), in_land)
    unpack_diag(early(store_of), in_diag_land, 2)

    def scale(p, m, r0, n):
        planes, rows = pl.ds(p, m), pl.ds(r0, n)
        k = k_f[planes, rows]
        for comp in range(3):
            va[comp, planes, rows] = k * ua[comp, planes, rows]

    def strips(act, p, m, low, high, n):
        act(p, m, low, n)
        act(p, m, high, n)

    strips(scale, own_plane, 8, 6, 40, 2)
    scale(halo_2, 2, 6, 36)
    strips(k_z, own_plane, 8, 6, 40, 2)
    k_z(halo_2, 2, 6, 36)
    strips(k_y, own_plane, 8, 7, 39, 2)
    k_y(halo_2, 2, 7, 34)
    strips(coefficients, all_but_1, 7, 7, 39, 2)
    coefficients(across_2, 2, 7, 34)
    strips(lambda p, m, r0, n: z_stage(ua, va, work, p, m, r0, n, fine_w, 1), own_plane, 8, 6, 40, 2)
    z_stage(ua, va, work, halo_2, 2, 6, 36, fine_w, 1)
    strips(lambda p, m, r0, n: y_stage(ua, work, p, m, r0, n), own_plane, 8, 7, 39, 2)
    y_stage(ua, work, halo_2, 2, 7, 34)
    strips(lambda p, m, r0, n: x_stage(ua, work, p, m, r0, n, first_sweep), all_but_1, 7, 7, 39, 2)
    x_stage(ua, work, across_2, 2, 7, 34, first_sweep)
    pack(rows_of_u1(load_of, ub), u_pack)
    pack_diag(rows_of_u1(load_of, ub), u_diag_pack, 3)
    start(M_U)
    strips(lambda p, m, r0, n: z_stage(ub, vb, work_2, p, m, r0, n, fine_w, 1), all_but_1, 7, 7, 39, 2)
    z_stage(ub, vb, work_2, across_2, 2, 7, 34, fine_w, 1)
    strips(lambda p, m, r0, n: y_stage(ub, work_2, p, m, r0, n), all_but_1, 7, 8, 38, 2)
    y_stage(ub, work_2, across_2, 2, 8, 32)
    strips(lambda p, m, r0, n: x_stage(ub, work_2, p, m, r0, n, to_residual), all_but_2, 6, 8, 38, 2)
    x_stage(ub, work_2, last_2, 2, 8, 32, to_residual)

    def put_target(dst, packed, depth):
        for comp in range(3):

            def put(half, value, comp=comp):
                dst[0, comp, half, pl.ds(8, 16)] = value

            halve(lambda p, rows, comp=comp: res[comp, own_plane + p, rows], 8, put)
            for half in range(2):
                at = pl.ds((2 * comp + half) * depth, depth)
                packed[0, at] = dst[0, comp, half, pl.ds(8, depth)]
                packed[1, at] = dst[0, comp, half, pl.ds(24 - depth, depth)]

    def far_target(dst, land, depth):
        for band in range(2):
            for comp in range(3):
                for half in range(2):
                    at = pl.ds((2 * comp + half) * depth, depth)
                    dst[band, comp, half, pl.ds(24, depth)] = land[0, band, at]
                    dst[band, comp, half, pl.ds(8 - depth, depth)] = land[1, band, at]

    put_target(t_1, t1_pack, 5)
    start(M_T)
    for comp in range(3):
        uc[comp, planes_own, own_rows] = ub[comp, planes_own, own_rows]
    start(M_FACE_U1)

    def repack(load, rows, emit):
        for half in range(2):
            low, high = load(b, half, rows), load(1 - b, half, rows)
            emit(1 + half, jnp.where(even, low, roll(high, 1)))
            emit(3 + half, jnp.where(even, roll(low, -1), high))

    def wrap_after(value):
        return jnp.where(even, roll(value, -1), 0.0)

    def wrap_before(value):
        return jnp.where(even, 0.0, roll(value, 1))

    received(M_LATE, M_LATE_K, M_LATE_FREE)
    unpack(late(store_of), late_land)
    unpack_diag(late_diag(store_of), late_diag_land, 3)
    for q in range(0, 11, CHUNK):
        size = min(CHUNK, 11 - q)
        k_z(1 + q, size, 5, 38)
        k_y(1 + q, size, 6, 36)
    coefficients(1 + b, 10, 6, 36)

    received(M_KC)

    def put_kq(q, value):
        k_q[q, pl.ds(2, 28)] = value

    repack(lambda slot, half, rows: kc[slot, half, rows], pl.ds(2, 28), put_kq)
    czu, ctv = coarse_work[0], coarse_work[6]
    for q in range(1, 5):
        k = k_q[q, pl.ds(2, 28)]
        left, right = z_pair(k, coarse_w, 2)
        czu[0, q, pl.ds(2, 28)] = k + (left + right)
    whole = pl.ds(3, 26)
    for q in range(1, 5):
        ctv[0, q, whole] = czu[0, q, whole] + 0.5 * (czu[0, q, pl.ds(2, 26)] + czu[0, q, pl.ds(4, 26)])
    ctv[0, 5, whole] = wrap_after(ctv[0, 1, whole])
    ctv[0, 0, whole] = wrap_before(ctv[0, 4, whole])
    for q in range(1, 5):
        k = k_q[q, whole]
        t = ctv[0, q, whole] + 0.5 * (ctv[0, q - 1, whole] + ctv[0, q + 1, whole])
        g_q[q, whole] = 32.0 * k + 4.0 * t
        s_q[q, whole] = jnp.where(k > 0.0, 0.15 / jnp.where(k > 0.0, 6.0 * k + t, 1.0), 0.0)

    def coarse_sweep(field, scaled, out_u, out_v, r0, n):
        z_stage(field, scaled, coarse_work, 1, 4, r0 - 1, n + 2, coarse_w, 2)
        y_stage(field, coarse_work, 1, 4, r0, n)
        cep, cem, _, ctv = coarse_work[3:]
        rows = pl.ds(r0, n)
        for comp in range(3):
            cep[comp, 5, rows] = wrap_after(cep[comp, 1, rows])
            cem[comp, 0, rows] = wrap_before(cem[comp, 4, rows])
            ctv[comp, 5, rows] = wrap_after(ctv[comp, 1, rows])
            ctv[comp, 0, rows] = wrap_before(ctv[comp, 4, rows])
        here = pl.ds(1, 4)
        k, g4, s = k_q[here, rows], g_q[here, rows], s_q[here, rows]
        for comp in range(3):
            terms = x_terms(field, k, g4, coarse_work, comp, 1, 4, rows)
            u = field[comp, here, rows] + (w_q[comp, here, rows] + s * terms)
            out_u[comp, here, rows] = u
            if out_v is not None:
                out_v[comp, here, rows] = u * k

    def coarse(target, r0, n):
        rows = pl.ds(r0, n)
        for comp in range(3):

            def put(q, value, comp=comp):
                w = 16.0 * s_q[q, rows] * value
                w_q[comp, q, rows] = w
                ca[comp, q, rows] = w
                cva[comp, q, rows] = w * k_q[q, rows]

            repack(lambda slot, half, at, comp=comp: target[slot, comp, half, at], rows, put)
        coarse_sweep(ca, cva, cb, cvb, r0 + 1, n - 2)
        coarse_sweep(cb, cvb, ca, cva, r0 + 2, n - 4)
        coarse_sweep(ca, cva, cb, None, r0 + 3, n - 6)
        last, count = r0 + 3, n - 6
        for comp in range(3):
            for q in range(1, 5):
                value = cb[comp, q, pl.ds(last, count)]
                for x, part in ((q - 1, jnp.where(even, value, roll(value, 1))), (q + 3, jnp.where(even, roll(value, -1), value))):
                    prolonged[comp, x, pl.ds(2 * last - 8, count, stride=2)] = part
                    prolonged[comp, x, pl.ds(2 * last - 7, count, stride=2)] = part

    def correct(field, out_u, out_v, p, m, r0, n):
        rows = pl.ds(r0, n)
        for q in range(m):
            at = p + q
            x = (at - 1 + 5 * b) // 2
            k, free = k_f[at, rows], free_f[at, rows]
            for comp in range(3):
                u = field[comp, at, rows] + free * prolonged[comp, x, rows]
                out_u[comp, at, rows] = u
                out_v[comp, at, rows] = u * k

    received(M_T)
    far_target(t_1, t1_land, 5)
    coarse(t_1, 3, 26)
    received(M_U)
    unpack(rows_of_u1(store_of, uc), u_land)
    unpack_diag(rows_of_u1(store_of, uc), u_diag_land, 3)
    correct(uc, ud, vd, own_plane, 8, 5, 38)

    def partner_planes():
        received(M_FACE_U1)
        correct(uc, ud, vd, 9 - 8 * b, 3, 5, 38)

    fine(ud, vd, 11, 10, 6, 36, sweep_to(ue, ve), (8, partner_planes))

    fine(ue, ve, 10, 9, 7, 34, sweep_to(ud, vd))
    fine(ud, vd, 9, 8, 8, 32, to_residual)
    put_target(t_2, t2_pack, 4)
    start(M_T2)
    received(M_T2)
    far_target(t_2, t2_land, 4)
    coarse(t_2, 4, 24)
    correct(ud, ue, ve, 1 + 2 * b, 9, 7, 34)
    fine(ue, ve, 9, 8, 8, 32, sweep_to(out_f, None))
    result = pltpu.make_async_copy(out_f.at[:, planes_own, own_rows], out_hbm, in_sem.at[3])
    result.start()
    sent(*range(MESSAGES))
    result.wait()


def solution(mesh):
    bricks = mesh.shape["brick"]

    def body(stiffness, prescribed, pinned):
        def f32(*shape):
            return pltpu.VMEM(shape, jnp.float32)

        one, three = f32(PLANES, ROWS, 128), f32(3, PLANES, ROWS, 128)
        q1, q3 = f32(6, COARSE_ROWS, 128), f32(3, 6, COARSE_ROWS, 128)
        scratch = [
            f32(3, 8, 32, 128),
            pltpu.VMEM((8, 32, 128), jnp.int32),
            f32(8, 32, 128),
            *[one] * 5,
            *[three] * 11,
            *[three] * 14,
            f32(3, PLANES, ROWS, 128),
            *[f32(2, 72, 128)] * 2,
            *[f32(2, 24, 128)] * 2,
            *[f32(2, 24, 128)] * 2,
            *[f32(2, 24, 128)] * 2,
            *[f32(2, 72, 128)] * 2,
            *[f32(2, 32, 128)] * 2,
            f32(2, 2, COARSE_ROWS, 128),
            *[f32(2, 3, 2, COARSE_ROWS, 128)] * 2,
            f32(2, 32, 128),
            f32(2, 2, 32, 128),
            f32(2, 24, 128),
            f32(2, 2, 24, 128),
            *[q1] * 3,
            *[q3] * 5,
            *[q3] * 7,
            pltpu.SemaphoreType.DMA((4,)),
            pltpu.SemaphoreType.DMA((MESSAGES, 5)),
            pltpu.SemaphoreType.DMA((MESSAGES, 5)),
        ]
        hbm = pl.BlockSpec(memory_space=pl.ANY)
        return pl.pallas_call(
            functools.partial(kernel, bricks),
            out_shape=jax.ShapeDtypeStruct(prescribed.shape, jnp.float32),
            in_specs=[hbm] * 3,
            out_specs=hbm,
            scratch_shapes=scratch,
            compiler_params=pltpu.CompilerParams(collective_id=0, has_side_effects=True, vmem_limit_bytes=58 * 2**20),
        )(stiffness, prescribed, pinned)

    return jax.shard_map(
        body,
        mesh=mesh,
        in_specs=(P("band", "brick", None), P(None, "band", "brick", None), P("band", "brick", None)),
        out_specs=P(None, "band", "brick", None),
        check_vma=False,
    )
```
